1024 devices in a mesh: home: 64 (over z, x), head: 16 (over y, core).
Axes of the slice: x: 8, y: 8, z: 8, core: 2. Of those that a mesh axis runs over, the one named last changes fastest.
Arguments:
- queries: bfloat16 [8192, 128, 576], P('home', 'head'), may hold values from -18 to 18
- leaf_kv: bfloat16 [8192, 576], P('home'), may hold values from -4.5 to 4.5
- grad_out: bfloat16 [8192, 128, 512], P('home', 'head'), may hold values from -4.5 to 4.5
- latent_pages: bfloat16 [3072, 64, 576], P('home', 'head'), may hold values from -5 to 5
- ancestor_home: int32 [512, 4], P('home'), may hold values from 0 to 63, all different within a row; in each aligned block of 8 rows (0 to 7, 8 to 15, ...) at most 2 rows name the same one
- ancestor_page: int32 [512, 4], P('home'), may hold values from 0 to 47
- ancestor_count: int32 [512], P('home'), may hold values from 1 to 4, as said below
Outputs:
- page_grads: float32 [3072, 64, 576], P('home', 'head')
- leaf_grads: float32 [8192, 576], P(('home', 'head'))
The draws below stay inside these ranges and needn't reach their ends.
Inputs may be any that keep to these rules, and one draw needn't show every extreme that they name: `ancestor_home`: each leaf names 4 different homes; the leaves of one device (aligned blocks of 8 leaves) name any one home at most 2 times, a bound that some block reaches. `ancestor_count`: in each aligned block of 8 leaves (one device's), exactly 4 leaves have 4 live ancestor pages and the others 1.
All inputs are finite; a program needn't handle non-finite values.
Results may differ from the reference program's by a relative error of at most 0.025.
Values may be sent and summed in bfloat16 or wider, within the bound.
No kernel may reach another device: no remote copies, remote signals or barrier semaphores. Data moves between devices by JAX's collectives and lax.ppermute only.
A program may use at most 64 MiB of HBM per device.

```python
import math
import jax
import jax.numpy as jnp
import numpy as np
from jax import lax

H = 128
LAT = 512
ROPE = 64
PAGE = 64
LEAF = 16
ANC = 4
LEAVES_DEV = 8
P_DEV = 48
HOMES = 64
TOKENS = 8192
LEAVES = 512
PAGES = 3072
CAP = 2
N_HEAD = 16


def draw_latent_pages(key, part):
    key = jax.random.fold_in(key, 11)
    shape_all = (PAGES, PAGE, LAT + ROPE)
    return jnp.clip(jax.random.normal(key, shape_all, jnp.float32), -4.5, 4.5).astype(jnp.bfloat16)


def draw_queries(key, part):
    key = jax.random.fold_in(key, 12)
    shape_all = (TOKENS, H, LAT + ROPE)
    return jnp.clip(jax.random.normal(key, shape_all, jnp.float32), -4.5, 4.5).astype(jnp.bfloat16)


def block_order(block_key):
    return jax.random.permutation(block_key, LEAVES_DEV)


def draw_ancestor_count(key, part):
    key = jax.random.fold_in(key, 13)
    block_keys = jax.random.split(key, LEAVES // LEAVES_DEV)
    orders = jax.vmap(block_order)(block_keys)
    counts = jnp.where(orders < LEAVES_DEV // 2, ANC, 1)
    return counts.reshape(LEAVES).astype(jnp.int32)


def with_ends(values, stream_key, low, high):
    longest = values.shape.index(max(values.shape))
    spots = []
    for shift in (0, 1):
        where = [jax.random.randint(jax.random.fold_in(stream_key, axis), (), 0, length) for axis, length in enumerate(values.shape)]
        where[longest] = (where[longest] + shift) % values.shape[longest]
        spots.append(tuple(where))
    return values.at[spots[0]].set(low).at[spots[1]].set(high)


def block_levels(stream_key, extent, cuts, smallest, top_value):
    def one(axis_at, parts):
        draws = jax.random.uniform(jax.random.fold_in(jax.random.fold_in(stream_key, 6), axis_at), (parts,), jnp.float32, smallest / len(cuts), top_value / len(cuts))
        return jnp.repeat(jnp.exp(draws), extent[axis_at] // parts).reshape((-1,) + (1,) * (len(extent) - axis_at - 1))

    level = one(*cuts[0])
    for cut in cuts[1:]:
        level = level * one(*cut)
    return level


def assign_block(key, own, number, rows, amount, top, bound, slope):
    sequence = jax.random.permutation(key, amount)
    packed, ordinary = shares(amount, rows * top, bound, slope, True), shares(amount, rows * top, bound, slope, False)
    places = jnp.arange(amount)

    def named(sizes, turn):
        used = int((sizes > 0).sum())
        fixed = max(1, used // 4)
        moved = fixed + (places - fixed + turn * (used - fixed)) % max(1, amount - fixed)
        return jnp.zeros((amount,), jnp.int32).at[sequence[jnp.where(places < fixed, places, moved)]].set(jnp.asarray(sizes, jnp.int32))

    sizes = jnp.where(number % 4 == 0, named(packed, number // 4), named(ordinary, number - number // 4 - 1))
    mixed = jax.random.permutation(jax.random.fold_in(own, 3), amount)
    source_of, receiver = mixed[0:amount // 2 * 2:2], mixed[1:amount // 2 * 2:2]
    slack = jnp.minimum(sizes[source_of] - 1, bound - sizes[receiver]) // 2
    slack = jnp.where((source_of == sequence[0]) | (receiver == sequence[0]) | (sizes[receiver] == 0), 0, jnp.maximum(slack, 0))
    moved = jax.random.randint(jax.random.fold_in(own, 4), (amount // 2,), 0, 1 << 20) % (slack + 1)
    sizes = sizes.at[source_of].add(-moved).at[receiver].add(moved)
    members = jnp.searchsorted(jnp.cumsum(sizes), jnp.arange(rows * top), side="right").astype(jnp.int32)
    table = members.reshape(top, rows).T
    table = table[jax.random.permutation(jax.random.fold_in(own, 1), rows)]
    turn = jax.random.randint(jax.random.fold_in(own, 2), (rows, 1), 0, top)
    return jnp.take_along_axis(table, (jnp.arange(top)[None, :] + turn) % top, axis=1)


def shares(number_of, total, most, skew, full):
    weights = [(1 << 20) // math.isqrt(standing ** skew) + 1 for standing in range(1, number_of + 1)]
    largest = most if full else min(most, max(-(-total // number_of), total * weights[0] // sum(weights)))
    least = 1 if total - largest >= number_of - 1 else 0
    given, rest = [largest] + [least] * (number_of - 1), total - largest - least * (number_of - 1)
    while rest > 0:
        candidates = [i for i in range(1, number_of) if given[i] < largest] or [i for i in range(1, number_of) if given[i] < most]
        mass, remaining = sum([weights[i] for i in candidates]), rest
        for i in candidates:
            extra = min(most - given[i], max(1, remaining * weights[i] // mass), rest)
            given[i] = given[i] + extra
            rest = rest - extra
    return np.array(given)


def gaussian(rng, extent, width, limit, cuts=(), dtype=jnp.bfloat16):
    array = jax.random.normal(rng, extent, jnp.float32) * width
    if len(cuts) > 0:
        array = block_levels(rng, extent, cuts, -0.22, 0.18) * array
    return jnp.clip(array, min=-limit, max=limit).astype(dtype)


def setup_inputs(seed: int = 0) -> dict:
    key_list = jax.random.split(jax.random.key(seed), 8)
    queries = draw_queries(jax.random.fold_in(key_list[7], 71), 0)
    leaf_kv = gaussian(key_list[1], (TOKENS, LAT + ROPE), 1.0, 4.5, ((0, 64),))
    grad_out = gaussian(key_list[2], (TOKENS, H, LAT), 1.0, 4.5, ((0, 64), (1, 16)))
    latent_pages = draw_latent_pages(jax.random.fold_in(key_list[7], 71), 0)
    ancestor_home_keys = jax.random.split(jax.random.fold_in(key_list[4], 1), LEAVES // LEAVES_DEV)
    ancestor_home_turns = jax.random.permutation(jax.random.fold_in(key_list[4], 3), LEAVES // LEAVES_DEV)
    ancestor_home = jax.vmap(lambda own, number: assign_block(jax.random.fold_in(key_list[4], 2), own, number, LEAVES_DEV, HOMES, ANC, CAP, 2))(ancestor_home_keys, ancestor_home_turns).reshape((LEAVES, ANC))
    ancestor_page = with_ends(jax.random.randint(key_list[5], (LEAVES, ANC), 0, P_DEV), jax.random.fold_in(key_list[5], 1), 0, P_DEV - 1).astype(jnp.int32)
    ancestor_count = draw_ancestor_count(jax.random.fold_in(key_list[7], 71), 0)
    return dict(queries=queries, leaf_kv=leaf_kv, grad_out=grad_out, latent_pages=latent_pages, ancestor_home=ancestor_home, ancestor_page=ancestor_page, ancestor_count=ancestor_count)


softmax_scale = 192.0 ** -0.5


def reference(queries, leaf_kv, grad_out, latent_pages, ancestor_home, ancestor_page, ancestor_count):
    key_width = LAT + ROPE
    page_span = ANC * PAGE
    group_size = H // N_HEAD
    page_ids = (ancestor_home * P_DEV + ancestor_page).astype(jnp.int32)
    query_blocks = queries.reshape(LEAVES, LEAF, H, key_width)
    grad_blocks = grad_out.reshape(LEAVES, LEAF, H, LAT)
    own_blocks = leaf_kv.reshape(LEAVES, LEAF, key_width)
    causal = jnp.arange(LEAF)[None, :] <= jnp.arange(LEAF)[:, None]

    def per_leaf(leaf_items):
        query_leaf, grad_leaf, own_keys, leaf_ids, live_count = leaf_items
        fetched = latent_pages[leaf_ids].reshape(page_span, key_width)
        key_rows = jnp.concatenate([fetched, own_keys], 0).astype(jnp.float32)
        query_wide = query_leaf.astype(jnp.float32)
        grad_wide = grad_leaf.astype(jnp.float32)
        scores = softmax_scale * jnp.einsum("ihd,kd->hik", query_wide, key_rows)
        page_live = (jnp.arange(page_span) // PAGE) < live_count
        key_mask = jnp.concatenate([jnp.broadcast_to(page_live[None, :], (LEAF, page_span)), causal], 1)
        scores = jnp.where(key_mask[None], scores, -jnp.inf)
        row_max = jnp.max(scores, -1, keepdims=True)
        raised = jnp.exp(scores - row_max)
        weights = raised / jnp.sum(raised, -1, keepdims=True)
        weights_b = lax.optimization_barrier(weights.astype(jnp.bfloat16)).astype(jnp.float32)
        grad_weights = jnp.einsum("ihc,kc->hik", grad_wide, key_rows[:, :LAT])
        row_delta = jnp.sum(weights * grad_weights, -1, keepdims=True)
        dscore = weights * (grad_weights - row_delta)
        dscore_b = lax.optimization_barrier(dscore.astype(jnp.bfloat16)).astype(jnp.float32)
        key_len = page_span + LEAF
        part_query = softmax_scale * jnp.einsum(
            "ghik,ighd->gkd",
            dscore_b.reshape(N_HEAD, group_size, LEAF, key_len),
            query_wide.reshape(LEAF, N_HEAD, group_size, key_width))
        part_value = jnp.einsum(
            "ghik,ighc->gkc",
            weights_b.reshape(N_HEAD, group_size, LEAF, key_len),
            grad_wide.reshape(LEAF, N_HEAD, group_size, LAT))
        group_parts = part_query + jnp.pad(part_value, ((0, 0), (0, 0), (0, ROPE)))
        group_parts = lax.optimization_barrier(group_parts.astype(jnp.bfloat16)).astype(jnp.float32)
        summed = jnp.sum(group_parts, 0)
        request_grads = summed[:page_span].astype(jnp.bfloat16).reshape(ANC, PAGE, key_width)
        return request_grads, summed[page_span:]

    request_grads, leaf_terms = lax.map(per_leaf, (query_blocks, grad_blocks, own_blocks, page_ids, ancestor_count))
    page_grads = jax.ops.segment_sum(
        request_grads.reshape(LEAVES * ANC, PAGE, key_width).astype(jnp.float32),
        page_ids.reshape(LEAVES * ANC), num_segments=PAGES)
    return page_grads, leaf_terms.reshape(TOKENS, key_width)
```

```python
import math

import jax
import jax.numpy as jnp
from jax import lax
from jax.experimental import pallas as pl
from jax.experimental.pallas import tpu as pltpu
from jax.sharding import Mesh
from jax.sharding import PartitionSpec as P

softmax_scale = 192.0 ** (-0.5)
BF16 = jnp.bfloat16
F32 = jnp.float32
HOME = ("z", "x")
TILE = 16


def attention_kernel(
    order_ref, core_ref, query_ref, grad_ref, mine_ref, other_ref, own_ref, out_mine, out_other
):
    step = pl.program_id(0)
    big_count = out_mine.shape[1] // TILE - 2
    planes, _, width = mine_ref.shape
    rows, latent = grad_ref.shape
    leaf_len = own_ref.shape[0]
    half = leaf_len // 2
    span = planes * TILE
    page_rows = 2 * span
    key_count = page_rows + leaf_len
    keys = jnp.concatenate(
        [mine_ref[...].reshape(span, width), other_ref[...].reshape(span, width), own_ref[...]], 0
    )
    grads = jnp.concatenate([grad_ref[...], jnp.zeros((rows, width - latent), BF16)], 1)
    stacked = jnp.concatenate([query_ref[...], grads], 0)
    products = lax.dot_general(
        keys, stacked, (((1,), (1,)), ((), ())), preferred_element_type=F32
    )
    scores = softmax_scale * products[:, :rows]
    grad_weights = products[:, rows:]
    key_at = lax.broadcasted_iota(jnp.int32, (key_count, rows), 0)
    token_at = lax.broadcasted_iota(jnp.int32, (key_count, rows), 1) // (rows // leaf_len)
    quarter = (key_at % TILE) // (TILE // 4)
    wanted = jnp.where(step < big_count, quarter, step - big_count)
    gap = jnp.where(
        key_at < page_rows, jnp.abs(quarter - wanted), jnp.maximum(key_at - page_rows - token_at, 0)
    )
    scores = jnp.where(gap == 0, scores, -jnp.inf)
    raised = jnp.exp(scores - jnp.max(scores, 0, keepdims=True))
    weights = raised / jnp.sum(raised, 0, keepdims=True)
    row_delta = jnp.sum(weights * grad_weights, 0, keepdims=True)
    dscore = weights * (grad_weights - row_delta)
    left = jnp.concatenate([(softmax_scale * dscore).astype(BF16), weights.astype(BF16)], 1)
    key_grads = lax.dot_general(
        left, stacked, (((1,), (0,)), ((), ())), preferred_element_type=F32
    )
    grads_mine = key_grads[:span].reshape(planes, TILE, width)
    grads_other = key_grads[span:page_rows].reshape(planes, TILE, width)

    @pl.when(step <= big_count)
    def _():
        spot = pl.ds(pl.multiple_of(step * TILE, TILE), TILE)
        out_mine[:, spot, :] = grads_mine.astype(BF16)
        out_other[:, spot, :] = grads_other.astype(BF16)

    @pl.when(step > big_count)
    def _():
        spot = pl.ds(big_count * TILE, TILE)
        out_mine[:, spot, :] = (out_mine[:, spot, :].astype(F32) + grads_mine).astype(BF16)
        out_other[:, spot, :] = (out_other[:, spot, :].astype(F32) + grads_other).astype(BF16)

    leaf = order_ref[step]
    first = core_ref[0] == 0
    low, high = key_grads[page_rows : page_rows + half], key_grads[page_rows + half :]
    tail = pl.ds((big_count + 1) * TILE, TILE)
    blank = jnp.zeros((TILE - half, width), F32)
    out_mine[leaf, tail, :] = jnp.concatenate([jnp.where(first, low, high), blank], 0).astype(BF16)
    out_other[leaf, tail, :] = jnp.concatenate([jnp.where(first, high, low), blank], 0).astype(BF16)


def attention(order, core, queries, grad_out, mine, other, leaf_kv):
    planes, live_rows, width = mine.shape
    leaf_count = order.shape[0]
    leaf_len = leaf_kv.shape[0] // leaf_count
    latent = grad_out.shape[1]
    rows = queries.shape[0] // leaf_count
    last = live_rows // TILE - 1
    out_shape = (planes, live_rows + TILE, width)
    whole = pl.BlockSpec(out_shape, lambda i, o, c: (0, 0, 0))
    by_leaf = lambda i, o, c: (o[i], 0)
    by_tile = lambda i, o, c: (0, jnp.minimum(i, last), 0)
    return pl.pallas_call(
        attention_kernel,
        grid_spec=pltpu.PrefetchScalarGridSpec(
            num_scalar_prefetch=2,
            grid=(leaf_count,),
            in_specs=[
                pl.BlockSpec((rows, width), by_leaf),
                pl.BlockSpec((rows, latent), by_leaf),
                pl.BlockSpec((planes, TILE, width), by_tile),
                pl.BlockSpec((planes, TILE, width), by_tile),
                pl.BlockSpec((leaf_len, width), by_leaf),
            ],
            out_specs=[whole, whole],
        ),
        out_shape=[jax.ShapeDtypeStruct(out_shape, BF16)] * 2,
        compiler_params=pltpu.CompilerParams(vmem_limit_bytes=32 * 1024 * 1024),
        name="attention",
    )(order, core, queries, grad_out, mine, other, leaf_kv)


def on_device(
    queries, leaf_kv, grad_out, latent_pages, ancestor_home, ancestor_page, ancestor_count
):
    z_count, x_count = lax.axis_size("z"), lax.axis_size("x")
    home_count = z_count * x_count
    tok_rows, head_local, key_width = queries.shape
    latent_width = grad_out.shape[2]
    leaf_count, anc_slots = ancestor_home.shape
    page_local, row_local = latent_pages.shape[:2]
    request_count = leaf_count * anc_slots
    capacity = 2
    slot_count = home_count * capacity
    big_count = leaf_count // 2
    live_count = big_count * anc_slots + leaf_count - big_count
    live_rows = live_count * row_local

    with jax.named_scope("plan"):
        leaf_at = jnp.arange(leaf_count)
        big = ancestor_count > 1
        before = leaf_at[None, :] < leaf_at[:, None]
        place = jnp.sum((before & (big[None, :] == big[:, None])).astype(jnp.int32), 1)
        place = jnp.where(big, place, big_count + place)
        order = jnp.sum(
            jnp.where(place[None, :] == leaf_at[:, None], leaf_at[None, :], 0), 1
        ).astype(jnp.int32)
        slot_at = jnp.arange(anc_slots)[None, :]
        live_at = jnp.where(
            big[:, None],
            place[:, None] * anc_slots + slot_at,
            big_count * anc_slots + place[:, None] - big_count,
        )
        live_at = jnp.where(slot_at < ancestor_count[:, None], live_at, -1).reshape(request_count)
        home_flat = ancestor_home.reshape(request_count)
        page_flat = ancestor_page.reshape(request_count)
        request_at = jnp.arange(request_count)
        earlier = (request_at[None, :] < request_at[:, None]) & (live_at[None, :] >= 0)
        rank = jnp.sum(((home_flat[None, :] == home_flat[:, None]) & earlier).astype(jnp.int32), 1)
        slot_of = jnp.where(live_at >= 0, home_flat * capacity + rank, -1)
        picked = slot_of[:, None] == jnp.arange(slot_count)[None, :]
        wanted = jnp.sum(jnp.where(picked, page_flat[:, None] + 1, 0), 0)
        chosen = live_at[None, :] == jnp.arange(live_count)[:, None]
        live_slot = jnp.sum(jnp.where(chosen, slot_of[None, :], 0), 1)
        row_at = jnp.arange(row_local)[None, :]
        live_slot_row = (live_slot[:, None] * row_local + row_at).reshape(live_rows)
        gather = (live_slot_row[:, None] == jnp.arange(slot_count * row_local)[None, :]).astype(BF16)

    with jax.named_scope("offsets"):
        incoming = lax.all_to_all(
            wanted.reshape(home_count, capacity), HOME, split_axis=0, concat_axis=0, tiled=True
        ).reshape(slot_count)
        wanted_row = jnp.where(
            incoming[:, None] > 0, (incoming[:, None] - 1) * row_local + row_at, -1
        ).reshape(slot_count * row_local)
        lookup = (
            wanted_row[:, None] == jnp.arange(page_local * row_local)[None, :]
        ).astype(BF16)

    with jax.named_scope("fetch"):
        pages = latent_pages.reshape(page_local * row_local, key_width)
        served = jnp.dot(lookup, pages, preferred_element_type=F32).astype(BF16)
        returned = lax.all_to_all(
            served.reshape(home_count, capacity * row_local, key_width),
            HOME, split_axis=0, concat_axis=0, tiled=True,
        ).reshape(slot_count * row_local, key_width)
        y_count = lax.axis_size("y")
        copies = jnp.dot(jnp.tile(gather, (y_count, 1)), returned, preferred_element_type=F32)
        copies = copies.astype(BF16).reshape(y_count, live_rows, key_width)

    with jax.named_scope("spread"):
        mine = lax.all_to_all(copies, "y", split_axis=0, concat_axis=0, tiled=True)
        swap = [(0, 1), (1, 0)]
        other = lax.ppermute(mine, "core", swap)

    with jax.named_scope("attend"):
        core = lax.axis_index("core").astype(jnp.int32).reshape(1)
        part_mine, part_other = attention(
            order,
            core,
            queries.reshape(tok_rows * head_local, key_width),
            grad_out.reshape(tok_rows * head_local, latent_width),
            mine,
            other,
            leaf_kv,
        )

    with jax.named_scope("collect"):
        from_core = lax.ppermute(part_other, "core", swap)
        pair = (part_mine.astype(F32) + from_core.astype(F32)).astype(BF16)
        parts = lax.all_to_all(pair, "y", split_axis=0, concat_axis=0, tiled=True)
        summed = jnp.sum(parts.astype(F32), 0)
        leaf_grads = summed[live_rows : live_rows + tok_rows // (2 * y_count)]
        request_grads = summed[:live_rows].astype(BF16)

    with jax.named_scope("home"):
        outbound = lax.dot_general(
            gather, request_grads, (((0,), (0,)), ((), ())), preferred_element_type=F32
        ).astype(BF16)
        arrived = lax.all_to_all(
            outbound.reshape(home_count, capacity * row_local, key_width),
            HOME, split_axis=0, concat_axis=0, tiled=True,
        ).reshape(slot_count * row_local, key_width)
        page_grads = lax.dot_general(
            lookup, arrived, (((0,), (0,)), ((), ())), preferred_element_type=F32
        )
    return (page_grads.reshape(page_local, row_local, key_width), leaf_grads)


def solution(mesh):
    home_count, head_count = mesh.devices.shape
    side = math.isqrt(home_count)
    split = Mesh(
        mesh.devices.reshape(side, home_count // side, head_count // 2, 2), ("z", "x", "y", "core")
    )
    head = ("y", "core")
    placed = (
        P(HOME, head, None),
        P(HOME, None),
        P(HOME, head, None),
        P(HOME, head, None),
        P(HOME, None),
        P(HOME, None),
        P(HOME),
    )
    return jax.shard_map(
        on_device,
        mesh=split,
        in_specs=placed,
        out_specs=(P(HOME, head, None), P(HOME + head, None)),
        check_vma=False,
    )
```

```python
import math

import jax
import jax.numpy as jnp
from jax import lax
from jax.experimental import pallas as pl
from jax.experimental.pallas import tpu as pltpu
from jax.sharding import Mesh
from jax.sharding import PartitionSpec as P

softmax_scale = 192.0 ** (-0.5)
BF16 = jnp.bfloat16
F32 = jnp.float32
HOME = ("z", "x")
CAPACITY = 2
TILE = 16
VMEM = pl.BlockSpec(memory_space=pltpu.VMEM)
SMEM = pl.BlockSpec(memory_space=pltpu.SMEM)
PARAMS = pltpu.CompilerParams(vmem_limit_bytes=32 * 1024 * 1024)


def iota(shape, dim):
    return lax.broadcasted_iota(jnp.int32, shape, dim)


def dot(a, b, contract):
    return lax.dot_general(a, b, ((contract[:1], contract[1:]), ((), ())), preferred_element_type=F32)


def plan_kernel(home_ref, page_ref, count_ref, order_ref, slot_ref, wanted_ref, seen):
    leaf_count, anc_slots = home_ref.shape
    half = leaf_count // 2
    set_size = 2 * anc_slots + 2
    live_count = slot_ref.shape[0] - 1
    for home in range(seen.shape[0]):
        seen[home] = 0
    row, column = iota(wanted_ref.shape, 0), iota(wanted_ref.shape, 1)
    wanted = jnp.zeros(wanted_ref.shape, jnp.int32)
    big_seen = small_seen = jnp.int32(0)
    for leaf in range(leaf_count):
        count = count_ref[leaf]
        big = jnp.where(count > 1, 1, 0)
        order_ref[jnp.where(big == 1, big_seen, half + small_seen)] = leaf
        big_at = (big_seen // 2) * set_size + (big_seen % 2) * anc_slots
        small_at = (small_seen // 2) * set_size + 2 * anc_slots + small_seen % 2
        first = jnp.where(big == 1, big_at, small_at)
        for slot in range(anc_slots):
            live = jnp.where(slot < count, 1, 0)
            home = home_ref[leaf, slot]
            rank = seen[home]
            seen[home] = rank + live
            slot_ref[jnp.where(live == 1, first + slot, live_count)] = home * CAPACITY + rank
            value = page_ref[leaf, slot] + 1
            at = jnp.where(live == 1, home * CAPACITY + rank, -1)
            wanted = jnp.where(row * CAPACITY + column == at, value, wanted)
        big_seen += big
        small_seen += 1 - big
    wanted_ref[...] = wanted


def lookup_of(incoming, row_local, page_rows):
    home_count = incoming.shape[0]
    slot_rows = home_count * CAPACITY * row_local
    per_home = CAPACITY * row_local
    spread = (iota((home_count, slot_rows), 1) // per_home == iota((home_count, slot_rows), 0)).astype(BF16)
    asked = dot(incoming.astype(F32).astype(BF16), spread, (0, 0)).astype(jnp.int32)
    column = iota((1, slot_rows), 1)
    asked = jnp.where((column % per_home) // row_local == 0, asked[:1], asked[1:])
    wanted_row = jnp.where(asked > 0, (asked - 1) * row_local + column % row_local, -1)
    return (iota((page_rows, slot_rows), 0) == wanted_row).astype(BF16)


def serve_kernel(row_local, incoming_ref, pages_ref, out_ref):
    lookup = lookup_of(incoming_ref[...], row_local, pages_ref.shape[0])
    out_ref[...] = dot(lookup, pages_ref[...], (0, 0)).astype(BF16).reshape(out_ref.shape)


def gather_of(slot_ref, row_local, slot_rows):
    live_count = slot_ref.shape[0] - 1
    shape = (live_count * row_local, slot_rows)
    row = iota((shape[0], 1), 0)
    target = jnp.zeros((shape[0], 1), jnp.int32)
    for at in range(live_count):
        target = jnp.where(row // row_local == at, slot_ref[at] * row_local, target)
    return (iota(shape, 1) == target + row % row_local).astype(BF16)


def compact_kernel(row_local, slot_ref, returned_ref, out_ref):
    slot_rows, width = returned_ref.shape
    chips, set_rows, _ = out_ref.shape
    fetched = dot(gather_of(slot_ref, row_local, slot_rows), returned_ref[...], (1, 0))
    sets = [fetched[:set_rows].astype(BF16), fetched[set_rows:].astype(BF16)]
    for chip in range(chips):
        out_ref[chip] = sets[chip % 2]


def pick_kernel(order_ref, query_ref, grad_ref, out_ref):
    latent, width = grad_ref.shape[2], query_ref.shape[2]
    out_ref[0, :, :latent] = grad_ref[0]
    blank = jnp.zeros((out_ref.shape[1], out_ref.shape[2] - latent - width), BF16)
    out_ref[0, :, latent:] = jnp.concatenate([query_ref[0], blank], 1)


def attention_kernel(
    order_ref, core_ref, query_ref, grad_ref, theirs_ref, mine_ref, other_ref, own_ref, out_mine, out_other
):
    chips, set_rows, width = mine_ref.shape
    rows, latent = grad_ref.shape[1:]
    leaf_len = own_ref.shape[0] // query_ref.shape[0]
    half = leaf_len // 2
    tail = set_rows - 2 * TILE
    page_rows = TILE // 4
    blank = jnp.zeros((2 * rows, width - latent), BF16)
    small = None
    leaf_tails = []
    for at in range(4):
        leaf = order_ref[at]
        span = TILE if at < 2 else tail
        start = at * TILE if at < 2 else 2 * TILE
        mine = mine_ref[:, start : start + span, :].reshape(chips * span, width)
        other = other_ref[:, start : start + span, :].reshape(chips * span, width)
        own_rows = pl.ds(pl.multiple_of(leaf * leaf_len, leaf_len), leaf_len)
        keys = jnp.concatenate([mine, other, own_ref[own_rows, :]], 0)
        paged = 2 * chips * span
        grads = jnp.concatenate([grad_ref[leaf], theirs_ref[at, :, :latent]], 0)
        stacked = jnp.concatenate(
            [query_ref[leaf], theirs_ref[at, :, latent : latent + width], jnp.concatenate([grads, blank], 1)], 0
        )
        products = dot(keys, stacked, (1, 1))
        key_at = iota((paged + leaf_len, 2 * rows), 0)
        token_at = iota((paged + leaf_len, 2 * rows), 1) % rows // (rows // leaf_len)
        strange = 0 if at < 2 else jnp.abs(key_at % tail // page_rows - (at - 2))
        gap = jnp.where(key_at < paged, strange, jnp.maximum(key_at - paged - token_at, 0))
        scores = jnp.where(gap == 0, softmax_scale * products[:, : 2 * rows], -jnp.inf)
        grad_weights = products[:, 2 * rows :]
        raised = jnp.exp(scores - jnp.max(scores, 0, keepdims=True))
        weights = raised / jnp.sum(raised, 0, keepdims=True)
        row_delta = jnp.sum(weights * grad_weights, 0, keepdims=True)
        dscore = softmax_scale * (weights * (grad_weights - row_delta))
        left = jnp.concatenate([dscore.astype(BF16), weights.astype(BF16)], 1)
        key_grads = dot(left, stacked, (1, 0))
        if at < 2:
            out_mine[:, start : start + span, :] = (
                key_grads[: chips * span].astype(BF16).reshape(chips, span, width)
            )
            out_other[:, start : start + span, :] = (
                key_grads[chips * span : paged].astype(BF16).reshape(chips, span, width)
            )
        else:
            small = key_grads[:paged] if small is None else small + key_grads[:paged]
        leaf_tails.append((leaf, key_grads[paged : paged + half], key_grads[paged + half :]))
    first = core_ref[0] == 0
    for chip in range(chips):
        low = high = jnp.zeros((half, width), F32)
        for leaf, leaf_low, leaf_high in leaf_tails:
            low = low + jnp.where(leaf == chip, leaf_low, 0.0)
            high = high + jnp.where(leaf == chip, leaf_high, 0.0)
        for out, part, rest in (
            (out_mine, small[: chips * tail], jnp.where(first, low, high)),
            (out_other, small[chips * tail :], jnp.where(first, high, low)),
        ):
            end = jnp.concatenate([part[chip * tail : (chip + 1) * tail], rest], 0)
            out[chip, 2 * TILE : 2 * TILE + tail + half, :] = end.astype(BF16)


def collect_kernel(row_local, slot_ref, parts_ref, out_ref, leaf_ref):
    chips, part_rows, width = parts_ref.shape
    set_rows = part_rows - leaf_ref.shape[0]
    sums = []
    for parity in range(2):
        total = parts_ref[parity].astype(F32)
        for chip in range(parity + 2, chips, 2):
            total = total + parts_ref[chip].astype(F32)
        sums.append(total)
    leaf_ref[...] = sums[0][set_rows:] + sums[1][set_rows:]
    requests = jnp.concatenate([sums[0][:set_rows], sums[1][:set_rows]], 0).astype(BF16)
    gather = gather_of(slot_ref, row_local, out_ref.shape[0])
    out_ref[...] = dot(gather, requests, (0, 0)).astype(BF16)


def return_kernel(row_local, incoming_ref, arrived_ref, out_ref):
    lookup = lookup_of(incoming_ref[...], row_local, out_ref.shape[0])
    out_ref[...] = dot(lookup, arrived_ref[...], (1, 0))


def call(kernel, name, out_shape, in_specs, out_specs, scratch=()):
    return pl.pallas_call(
        kernel, name=name, out_shape=out_shape, in_specs=in_specs, out_specs=out_specs,
        scratch_shapes=list(scratch), compiler_params=PARAMS,
    )


def on_device(
    queries, leaf_kv, grad_out, latent_pages, ancestor_home, ancestor_page, ancestor_count
):
    home_count = lax.axis_size("z") * lax.axis_size("x")
    chips = lax.axis_size("y")
    parity = lax.axis_index("y") % 2
    core = lax.axis_index("core").astype(jnp.int32).reshape(1)
    tok_rows, head_local, width = queries.shape
    latent = grad_out.shape[2]
    leaf_count, anc_slots = ancestor_home.shape
    leaf_len = tok_rows // leaf_count
    page_local, row_local = latent_pages.shape[:2]
    live_count = leaf_count // 2 * (anc_slots + 1)
    set_rows = live_count // 2 * row_local
    slot_rows = home_count * CAPACITY * row_local
    block_rows = leaf_len * head_local
    pair_width = -(-(latent + width) // 128) * 128
    swap = [(0, 1), (1, 0)]
    neighbours = [(i, i ^ 1) for i in range(chips)]
    shape = jax.ShapeDtypeStruct

    with jax.named_scope("plan"):
        order, slots, wanted = call(
            plan_kernel, "plan",
            [
                shape((leaf_count,), jnp.int32),
                shape((live_count + 1,), jnp.int32),
                shape((home_count, CAPACITY), jnp.int32),
            ],
            [SMEM, SMEM, SMEM], [SMEM, SMEM, VMEM], [pltpu.SMEM((home_count,), jnp.int32)],
        )(ancestor_home, ancestor_page, ancestor_count)
        sets = order.reshape(2, 2, 2).transpose(1, 0, 2).reshape(2, 4)
        kept, given = jnp.where(parity == 0, sets, sets[::-1])

    with jax.named_scope("offsets"):
        incoming = lax.all_to_all(wanted, HOME, split_axis=0, concat_axis=0, tiled=True)

    with jax.named_scope("pair"):
        leaf_queries = queries.reshape(leaf_count, block_rows, width)
        leaf_grad_out = grad_out.reshape(leaf_count, block_rows, latent)
        leaving = pl.pallas_call(
            pick_kernel,
            grid_spec=pltpu.PrefetchScalarGridSpec(
                num_scalar_prefetch=1,
                grid=(given.shape[0],),
                in_specs=[
                    pl.BlockSpec((1, block_rows, width), lambda i, o: (o[i], 0, 0)),
                    pl.BlockSpec((1, block_rows, latent), lambda i, o: (o[i], 0, 0)),
                ],
                out_specs=pl.BlockSpec((1, block_rows, pair_width), lambda i, o: (i, 0, 0)),
            ),
            out_shape=shape((given.shape[0], block_rows, pair_width), BF16),
            compiler_params=PARAMS,
            name="pick",
        )(given, leaf_queries, leaf_grad_out)
        theirs = lax.ppermute(leaving, "y", neighbours)

    with jax.named_scope("fetch"):
        served = call(
            lambda *refs: serve_kernel(row_local, *refs), "serve",
            shape((home_count, CAPACITY * row_local, width), BF16), [VMEM, VMEM], VMEM,
        )(incoming, latent_pages.reshape(page_local * row_local, width))
        returned = lax.all_to_all(served, HOME, split_axis=0, concat_axis=0, tiled=True)
        leaving_pages = call(
            lambda *refs: compact_kernel(row_local, *refs), "compact",
            shape((chips, set_rows, width), BF16), [SMEM, VMEM], VMEM,
        )(slots, returned.reshape(slot_rows, width))

    with jax.named_scope("spread"):
        mine = lax.all_to_all(leaving_pages, "y", split_axis=0, concat_axis=0, tiled=True)
        other = lax.ppermute(mine, "core", swap)

    with jax.named_scope("attend"):
        part_shape = shape((chips, set_rows + leaf_len // 2, width), BF16)
        part_mine, part_other = call(
            attention_kernel, "attention", [part_shape] * 2, [SMEM] * 2 + [VMEM] * 6, [VMEM] * 2
        )(kept, core, leaf_queries, leaf_grad_out, theirs, mine, other, leaf_kv)

    with jax.named_scope("collect"):
        from_core = lax.ppermute(part_other, "core", swap)
        both = (part_mine.astype(F32) + from_core.astype(F32)).astype(BF16)
        parts = lax.all_to_all(both, "y", split_axis=0, concat_axis=0, tiled=True)
        outbound, leaf_grads = call(
            lambda *refs: collect_kernel(row_local, *refs), "collect",
            [shape((slot_rows, width), BF16), shape((leaf_len // 2, width), F32)],
            [SMEM, VMEM], [VMEM, VMEM],
        )(slots, parts)

    with jax.named_scope("home"):
        arrived = lax.all_to_all(
            outbound.reshape(home_count, CAPACITY * row_local, width),
            HOME, split_axis=0, concat_axis=0, tiled=True,
        )
        page_grads = call(
            lambda *refs: return_kernel(row_local, *refs), "return",
            shape((page_local * row_local, width), F32), [VMEM, VMEM], VMEM,
        )(incoming, arrived.reshape(slot_rows, width))
    return (page_grads.reshape(page_local, row_local, width), leaf_grads)


def solution(mesh):
    home_count, head_count = mesh.devices.shape
    side = math.isqrt(home_count)
    split = Mesh(
        mesh.devices.reshape(side, home_count // side, head_count // 2, 2), ("z", "x", "y", "core")
    )
    head = ("y", "core")
    placed = (
        P(HOME, head, None),
        P(HOME, None),
        P(HOME, head, None),
        P(HOME, head, None),
        P(HOME, None),
        P(HOME, None),
        P(HOME),
    )
    return jax.shard_map(
        on_device,
        mesh=split,
        in_specs=placed,
        out_specs=(P(HOME, head, None), P(HOME + head, None)),
        check_vma=False,
    )
```

```python
import math

import jax
import jax.numpy as jnp
from jax import lax
from jax.experimental import pallas as pl
from jax.experimental.pallas import tpu as pltpu
from jax.sharding import Mesh
from jax.sharding import PartitionSpec as P

softmax_scale = 192.0 ** (-0.5)
BF16 = jnp.bfloat16
F32 = jnp.float32
HOME = ("z", "x")
CAPACITY = 2
TILE = 16
VMEM = pl.BlockSpec(memory_space=pltpu.VMEM)
SMEM = pl.BlockSpec(memory_space=pltpu.SMEM)
PARAMS = pltpu.CompilerParams(vmem_limit_bytes=32 * 1024 * 1024)


def iota(shape, dim):
    return lax.broadcasted_iota(jnp.int32, shape, dim)


def dot(a, b, contract):
    return lax.dot_general(a, b, ((contract[:1], contract[1:]), ((), ())), preferred_element_type=F32)


def plan_kernel(
    parity_ref, home_hbm, page_hbm, count_hbm, kept_ref, given_ref, slot_ref, wanted_ref, seen,
    home_ref, page_ref, count_ref, sems,
):
    copies = [
        pltpu.make_async_copy(source, target, sems.at[at])
        for at, (source, target) in enumerate(
            ((home_hbm, home_ref), (page_hbm, page_ref), (count_hbm, count_ref))
        )
    ]
    for copy in copies:
        copy.start()
    for home in range(seen.shape[0]):
        seen[home] = 0
    for copy in copies:
        copy.wait()
    anc_slots, leaf_count = home_ref.shape
    set_size = 2 * anc_slots + 2
    live_count = slot_ref.shape[0] - 1
    spare = kept_ref.shape[0] - 1
    row, column = iota(wanted_ref.shape, 0), iota(wanted_ref.shape, 1)
    wanted = jnp.zeros(wanted_ref.shape, jnp.int32)
    big_seen = small_seen = jnp.int32(0)
    for leaf in range(leaf_count):
        count = count_ref[leaf]
        big = jnp.where(count > 1, 1, 0)
        set_at = jnp.where(big == 1, big_seen // 2, small_seen // 2)
        place = jnp.where(big == 1, big_seen % 2, 2 + small_seen % 2)
        keep = set_at == parity_ref[0]
        kept_ref[jnp.where(keep, place, spare)] = leaf
        given_ref[jnp.where(keep, spare, place)] = leaf
        first = set_at * set_size + jnp.where(
            big == 1, place * anc_slots, 2 * anc_slots + small_seen % 2
        )
        for slot in range(anc_slots):
            live = jnp.where(slot < count, 1, 0)
            home = home_ref[slot, leaf]
            rank = seen[home]
            seen[home] = rank + live
            slot_ref[jnp.where(live == 1, first + slot, live_count)] = home * CAPACITY + rank
            value = page_ref[slot, leaf] + 1
            at = jnp.where(live == 1, home * CAPACITY + rank, -1)
            wanted = jnp.where(row * CAPACITY + column == at, value, wanted)
        big_seen += big
        small_seen += 1 - big
    wanted_ref[...] = wanted


def lookup_of(incoming, row_local, page_rows):
    home_count = incoming.shape[0]
    slot_rows = home_count * CAPACITY * row_local
    per_home = CAPACITY * row_local
    spread = (iota((home_count, slot_rows), 1) // per_home == iota((home_count, slot_rows), 0)).astype(BF16)
    asked = dot(incoming.astype(F32).astype(BF16), spread, (0, 0)).astype(jnp.int32)
    column = iota((1, slot_rows), 1)
    asked = jnp.where((column % per_home) // row_local == 0, asked[:1], asked[1:])
    wanted_row = jnp.where(asked > 0, (asked - 1) * row_local + column % row_local, -1)
    return (iota((page_rows, slot_rows), 0) == wanted_row).astype(BF16)


def serve_kernel(row_local, incoming_ref, pages_ref, out_ref):
    lookup = lookup_of(incoming_ref[...], row_local, pages_ref.shape[0])
    out_ref[...] = dot(lookup, pages_ref[...], (0, 0)).astype(BF16).reshape(out_ref.shape)


def gather_of(slot_ref, row_local, slot_rows):
    live_count = slot_ref.shape[0] - 1
    shape = (live_count * row_local, slot_rows)
    row = iota((shape[0], 1), 0)
    target = jnp.zeros((shape[0], 1), jnp.int32)
    for at in range(live_count):
        target = jnp.where(row // row_local == at, slot_ref[at] * row_local, target)
    return (iota(shape, 1) == target + row % row_local).astype(BF16)


def compact_kernel(row_local, slot_ref, returned_ref, out_ref):
    slot_rows, width = returned_ref.shape
    chips, set_rows, _ = out_ref.shape
    fetched = dot(gather_of(slot_ref, row_local, slot_rows), returned_ref[...], (1, 0))
    sets = [fetched[:set_rows].astype(BF16), fetched[set_rows:].astype(BF16)]
    for chip in range(chips):
        out_ref[chip] = sets[chip % 2]


def pick_kernel(order_ref, query_ref, grad_ref, out_ref):
    latent, width = grad_ref.shape[2], query_ref.shape[2]
    out_ref[0, :, :latent] = grad_ref[0]
    blank = jnp.zeros((out_ref.shape[1], out_ref.shape[2] - latent - width), BF16)
    out_ref[0, :, latent:] = jnp.concatenate([query_ref[0], blank], 1)


def attention_kernel(
    order_ref, core_ref, query_ref, grad_ref, theirs_ref, mine_ref, other_ref, own_ref, out_mine, out_other
):
    chips, set_rows, width = mine_ref.shape
    rows, latent = grad_ref.shape[1:]
    leaf_len = own_ref.shape[0] // query_ref.shape[0]
    half = leaf_len // 2
    tail = set_rows - 2 * TILE
    page_rows = TILE // 4
    blank = jnp.zeros((2 * rows, width - latent), BF16)
    small = None
    leaf_tails = []
    for at in range(4):
        leaf = order_ref[at]
        span = TILE if at < 2 else tail
        start = at * TILE if at < 2 else 2 * TILE
        mine = mine_ref[:, start : start + span, :].reshape(chips * span, width)
        other = other_ref[:, start : start + span, :].reshape(chips * span, width)
        own_rows = pl.ds(pl.multiple_of(leaf * leaf_len, leaf_len), leaf_len)
        keys = jnp.concatenate([mine, other, own_ref[own_rows, :]], 0)
        paged = 2 * chips * span
        grads = jnp.concatenate([grad_ref[leaf], theirs_ref[at, :, :latent]], 0)
        stacked = jnp.concatenate(
            [query_ref[leaf], theirs_ref[at, :, latent : latent + width], jnp.concatenate([grads, blank], 1)], 0
        )
        products = dot(keys, stacked, (1, 1))
        key_at = iota((paged + leaf_len, 2 * rows), 0)
        token_at = iota((paged + leaf_len, 2 * rows), 1) % rows // (rows // leaf_len)
        strange = 0 if at < 2 else jnp.abs(key_at % tail // page_rows - (at - 2))
        gap = jnp.where(key_at < paged, strange, jnp.maximum(key_at - paged - token_at, 0))
        scores = jnp.where(gap == 0, softmax_scale * products[:, : 2 * rows], -jnp.inf)
        grad_weights = products[:, 2 * rows :]
        raised = jnp.exp(scores - jnp.max(scores, 0, keepdims=True))
        weights = raised / jnp.sum(raised, 0, keepdims=True)
        row_delta = jnp.sum(weights * grad_weights, 0, keepdims=True)
        dscore = softmax_scale * (weights * (grad_weights - row_delta))
        left = jnp.concatenate([dscore.astype(BF16), weights.astype(BF16)], 1)
        key_grads = dot(left, stacked, (1, 0))
        if at < 2:
            out_mine[:, start : start + span, :] = (
                key_grads[: chips * span].astype(BF16).reshape(chips, span, width)
            )
            out_other[:, start : start + span, :] = (
                key_grads[chips * span : paged].astype(BF16).reshape(chips, span, width)
            )
        else:
            small = key_grads[:paged] if small is None else small + key_grads[:paged]
        leaf_tails.append((leaf, key_grads[paged : paged + half], key_grads[paged + half :]))
    first = core_ref[0] == 0
    for chip in range(chips):
        low = high = jnp.zeros((half, width), F32)
        for leaf, leaf_low, leaf_high in leaf_tails:
            low = low + jnp.where(leaf == chip, leaf_low, 0.0)
            high = high + jnp.where(leaf == chip, leaf_high, 0.0)
        for out, part, rest in (
            (out_mine, small[: chips * tail], jnp.where(first, low, high)),
            (out_other, small[chips * tail :], jnp.where(first, high, low)),
        ):
            end = jnp.concatenate([part[chip * tail : (chip + 1) * tail], rest], 0)
            out[chip, 2 * TILE : 2 * TILE + tail + half, :] = end.astype(BF16)


def collect_kernel(row_local, slot_ref, parts_ref, out_ref, leaf_ref):
    chips, part_rows, width = parts_ref.shape
    set_rows = part_rows - leaf_ref.shape[0]
    sums = []
    for parity in range(2):
        total = parts_ref[parity].astype(F32)
        for chip in range(parity + 2, chips, 2):
            total = total + parts_ref[chip].astype(F32)
        sums.append(total)
    leaf_ref[...] = sums[0][set_rows:] + sums[1][set_rows:]
    requests = jnp.concatenate([sums[0][:set_rows], sums[1][:set_rows]], 0).astype(BF16)
    gather = gather_of(slot_ref, row_local, out_ref.shape[0])
    out_ref[...] = dot(gather, requests, (0, 0)).astype(BF16)


def return_kernel(row_local, incoming_ref, arrived_ref, out_ref):
    lookup = lookup_of(incoming_ref[...], row_local, out_ref.shape[0])
    out_ref[...] = dot(lookup, arrived_ref[...], (1, 0))


def call(kernel, name, out_shape, in_specs, out_specs, scratch=()):
    return pl.pallas_call(
        kernel, name=name, out_shape=out_shape, in_specs=in_specs, out_specs=out_specs,
        scratch_shapes=list(scratch), compiler_params=PARAMS,
    )


def on_device(
    queries, leaf_kv, grad_out, latent_pages, ancestor_home, ancestor_page, ancestor_count
):
    home_count = lax.axis_size("z") * lax.axis_size("x")
    chips = lax.axis_size("y")
    parity = (lax.axis_index("y") % 2).astype(jnp.int32).reshape(1)
    core = lax.axis_index("core").astype(jnp.int32).reshape(1)
    tok_rows, head_local, width = queries.shape
    latent = grad_out.shape[2]
    leaf_count, anc_slots = ancestor_home.shape
    leaf_len = tok_rows // leaf_count
    page_local, row_local = latent_pages.shape[:2]
    live_count = leaf_count // 2 * (anc_slots + 1)
    set_rows = live_count // 2 * row_local
    slot_rows = home_count * CAPACITY * row_local
    block_rows = leaf_len * head_local
    pair_width = -(-(latent + width) // 128) * 128
    swap = [(0, 1), (1, 0)]
    neighbours = [(i, i ^ 1) for i in range(chips)]
    shape = jax.ShapeDtypeStruct

    with jax.named_scope("plan"):
        half = leaf_count // 2
        kept, given, slots, wanted = pl.pallas_call(
            plan_kernel,
            name="plan",
            in_specs=[SMEM] + [pl.BlockSpec(memory_space=pl.ANY)] * 3,
            out_specs=[SMEM, SMEM, SMEM, VMEM],
            out_shape=[
                shape((half + 1,), jnp.int32),
                shape((half + 1,), jnp.int32),
                shape((live_count + 1,), jnp.int32),
                shape((home_count, CAPACITY), jnp.int32),
            ],
            scratch_shapes=[
                pltpu.SMEM((home_count,), jnp.int32),
                pltpu.SMEM((anc_slots, leaf_count), jnp.int32),
                pltpu.SMEM((anc_slots, leaf_count), jnp.int32),
                pltpu.SMEM((leaf_count,), jnp.int32),
                pltpu.SemaphoreType.DMA((3,)),
            ],
            compiler_params=pltpu.CompilerParams(vmem_limit_bytes=56 * 1024 * 1024),
        )(parity, ancestor_home.T, ancestor_page.T, ancestor_count)

    with jax.named_scope("offsets"):
        incoming = lax.all_to_all(wanted, HOME, split_axis=0, concat_axis=0, tiled=True)

    with jax.named_scope("pair"):
        leaf_queries = queries.reshape(leaf_count, block_rows, width)
        leaf_grad_out = grad_out.reshape(leaf_count, block_rows, latent)
        leaving = pl.pallas_call(
            pick_kernel,
            grid_spec=pltpu.PrefetchScalarGridSpec(
                num_scalar_prefetch=1,
                grid=(half,),
                in_specs=[
                    pl.BlockSpec((1, block_rows, width), lambda i, o: (o[i], 0, 0)),
                    pl.BlockSpec((1, block_rows, latent), lambda i, o: (o[i], 0, 0)),
                ],
                out_specs=pl.BlockSpec((1, block_rows, pair_width), lambda i, o: (i, 0, 0)),
            ),
            out_shape=shape((half, block_rows, pair_width), BF16),
            compiler_params=pltpu.CompilerParams(vmem_limit_bytes=56 * 1024 * 1024),
            name="pick",
        )(given, leaf_queries, leaf_grad_out)
        pages = latent_pages.reshape(page_local * row_local, width)
        pages, leaving = lax.optimization_barrier((pages, leaving))
        theirs = lax.ppermute(leaving, "y", neighbours)

    with jax.named_scope("fetch"):
        served = call(
            lambda *refs: serve_kernel(row_local, *refs), "serve",
            shape((home_count, CAPACITY * row_local, width), BF16), [VMEM, VMEM], VMEM,
        )(incoming, pages)
        returned = lax.all_to_all(served, HOME, split_axis=0, concat_axis=0, tiled=True)
        leaving_pages = call(
            lambda *refs: compact_kernel(row_local, *refs), "compact",
            shape((chips, set_rows, width), BF16), [SMEM, VMEM], VMEM,
        )(slots, returned.reshape(slot_rows, width))

    with jax.named_scope("spread"):
        mine = lax.all_to_all(leaving_pages, "y", split_axis=0, concat_axis=0, tiled=True)
        other = lax.ppermute(mine, "core", swap)

    with jax.named_scope("attend"):
        part_shape = shape((chips, set_rows + leaf_len // 2, width), BF16)
        part_mine, part_other = call(
            attention_kernel, "attention", [part_shape] * 2, [SMEM] * 2 + [VMEM] * 6, [VMEM] * 2
        )(kept, core, leaf_queries, leaf_grad_out, theirs, mine, other, leaf_kv)

    with jax.named_scope("collect"):
        from_core = lax.ppermute(part_other, "core", swap)
        both = (part_mine.astype(F32) + from_core.astype(F32)).astype(BF16)
        parts = lax.all_to_all(both, "y", split_axis=0, concat_axis=0, tiled=True)
        outbound, leaf_grads = call(
            lambda *refs: collect_kernel(row_local, *refs), "collect",
            [shape((slot_rows, width), BF16), shape((leaf_len // 2, width), F32)],
            [SMEM, VMEM], [VMEM, VMEM],
        )(slots, parts)

    with jax.named_scope("home"):
        arrived = lax.all_to_all(
            outbound.reshape(home_count, CAPACITY * row_local, width),
            HOME, split_axis=0, concat_axis=0, tiled=True,
        )
        page_grads = call(
            lambda *refs: return_kernel(row_local, *refs), "return",
            shape((page_local * row_local, width), F32), [VMEM, VMEM], VMEM,
        )(incoming, arrived.reshape(slot_rows, width))
    return (page_grads.reshape(page_local, row_local, width), leaf_grads)


def solution(mesh):
    home_count, head_count = mesh.devices.shape
    side = math.isqrt(home_count)
    split = Mesh(
        mesh.devices.reshape(side, home_count // side, head_count // 2, 2), ("z", "x", "y", "core")
    )
    head = ("y", "core")
    placed = (
        P(HOME, head, None),
        P(HOME, None),
        P(HOME, head, None),
        P(HOME, head, None),
        P(HOME, None),
        P(HOME, None),
        P(HOME),
    )
    return jax.shard_map(
        on_device,
        mesh=split,
        in_specs=placed,
        out_specs=(P(HOME, head, None), P(HOME + head, None)),
        check_vma=False,
    )
```

```python
import math

import jax
import jax.numpy as jnp
from jax import lax
from jax.experimental import pallas as pl
from jax.experimental.pallas import tpu as pltpu
from jax.sharding import Mesh
from jax.sharding import PartitionSpec as P

softmax_scale = 192.0 ** (-0.5)
BF16 = jnp.bfloat16
F32 = jnp.float32
HOME = ("z", "xh", "xl")
PAIRS = ("z", "xh")
CAPACITY = 2
TILE = 16
VMEM = pl.BlockSpec(memory_space=pltpu.VMEM)
SMEM = pl.BlockSpec(memory_space=pltpu.SMEM)
PARAMS = pltpu.CompilerParams(vmem_limit_bytes=32 * 1024 * 1024)


def iota(shape, dim):
    return lax.broadcasted_iota(jnp.int32, shape, dim)


def dot(a, b, contract):
    return lax.dot_general(a, b, ((contract[:1], contract[1:]), ((), ())), preferred_element_type=F32)


def plan_kernel(
    parity_ref, home_hbm, page_hbm, count_hbm, kept_ref, given_ref, slot_ref, wanted_ref, seen,
    home_ref, page_ref, count_ref, sems,
):
    copies = [
        pltpu.make_async_copy(source, target, sems.at[at])
        for at, (source, target) in enumerate(
            ((home_hbm, home_ref), (page_hbm, page_ref), (count_hbm, count_ref))
        )
    ]
    for copy in copies:
        copy.start()
    for home in range(seen.shape[0]):
        seen[home] = 0
    for copy in copies:
        copy.wait()
    anc_slots, leaf_count = home_ref.shape
    set_size = 2 * anc_slots + 2
    live_count = slot_ref.shape[0] - 1
    spare = kept_ref.shape[0] - 1
    row, column = iota(wanted_ref.shape, 0), iota(wanted_ref.shape, 1)
    wanted = jnp.zeros(wanted_ref.shape, jnp.int32)
    big_seen = small_seen = jnp.int32(0)
    for leaf in range(leaf_count):
        count = count_ref[leaf]
        big = jnp.where(count > 1, 1, 0)
        set_at = jnp.where(big == 1, big_seen // 2, small_seen // 2)
        place = jnp.where(big == 1, big_seen % 2, 2 + small_seen % 2)
        keep = set_at == parity_ref[0]
        kept_ref[jnp.where(keep, place, spare)] = leaf
        given_ref[jnp.where(keep, spare, place)] = leaf
        first = set_at * set_size + jnp.where(
            big == 1, place * anc_slots, 2 * anc_slots + small_seen % 2
        )
        for slot in range(anc_slots):
            live = jnp.where(slot < count, 1, 0)
            home = home_ref[slot, leaf]
            rank = seen[home]
            seen[home] = rank + live
            slot_ref[jnp.where(live == 1, first + slot, live_count)] = home * CAPACITY + rank
            value = page_ref[slot, leaf] + 1
            at = jnp.where(live == 1, home * CAPACITY + rank, -1)
            wanted = jnp.where(row * wanted_ref.shape[1] + column == at, value, wanted)
        big_seen += big
        small_seen += 1 - big
    wanted_ref[...] = wanted


def asked_of(incoming, slot_rows, row_local):
    peers, lanes = incoming.shape
    shape = (peers, slot_rows)
    peer_rows = lanes * row_local
    spread = (iota(shape, 1) // peer_rows == iota(shape, 0)).astype(BF16)
    return dot(incoming.astype(F32).astype(BF16), spread, (0, 0)).astype(jnp.int32)


def serve_kernel(row_local, low_ref, incoming_ref, pages_ref, neighbour_ref, out_ref):
    page_rows = pages_ref.shape[0]
    peers, lanes = incoming_ref.shape
    slot_rows = peers * lanes * row_local
    asked = asked_of(incoming_ref[...], slot_rows, row_local)
    column = iota((1, slot_rows), 1)
    lane = column // row_local % lanes
    page = asked[:1]
    for at in range(1, lanes):
        page = jnp.where(lane == at, asked[at : at + 1], page)
    base = jnp.where(lane // CAPACITY == low_ref[0], 0, page_rows)
    wanted_row = jnp.where(page > 0, base + (page - 1) * row_local + column % row_local, -1)
    lookup = (iota((2 * page_rows, slot_rows), 0) == wanted_row).astype(BF16)
    pages = jnp.concatenate([pages_ref[...], neighbour_ref[...]], 0)
    out_ref[...] = dot(lookup, pages, (0, 0)).astype(BF16).reshape(out_ref.shape)


def gather_of(slot_ref, row_local, slot_rows):
    live_count = slot_ref.shape[0] - 1
    shape = (live_count * row_local, slot_rows)
    row = iota((shape[0], 1), 0)
    target = jnp.zeros((shape[0], 1), jnp.int32)
    for at in range(live_count):
        target = jnp.where(row // row_local == at, slot_ref[at] * row_local, target)
    return (iota(shape, 1) == target + row % row_local).astype(BF16)


def compact_kernel(row_local, slot_ref, returned_ref, out_ref):
    slot_rows, width = returned_ref.shape
    chips, set_rows, _ = out_ref.shape
    fetched = dot(gather_of(slot_ref, row_local, slot_rows), returned_ref[...], (1, 0))
    sets = [fetched[:set_rows].astype(BF16), fetched[set_rows:].astype(BF16)]
    for chip in range(chips):
        out_ref[chip] = sets[chip % 2]


def pick_kernel(order_ref, query_ref, grad_ref, out_ref):
    latent, width = grad_ref.shape[2], query_ref.shape[2]
    out_ref[0, :, :latent] = grad_ref[0]
    blank = jnp.zeros((out_ref.shape[1], out_ref.shape[2] - latent - width), BF16)
    out_ref[0, :, latent:] = jnp.concatenate([query_ref[0], blank], 1)


def attention_kernel(
    order_ref, core_ref, query_ref, grad_ref, theirs_ref, mine_ref, other_ref, own_ref, out_mine, out_other
):
    chips, set_rows, width = mine_ref.shape
    rows, latent = grad_ref.shape[1:]
    leaf_len = own_ref.shape[0] // query_ref.shape[0]
    half = leaf_len // 2
    tail = set_rows - 2 * TILE
    page_rows = TILE // 4
    blank = jnp.zeros((2 * rows, width - latent), BF16)
    small = None
    leaf_tails = []
    for at in range(4):
        leaf = order_ref[at]
        span = TILE if at < 2 else tail
        start = at * TILE if at < 2 else 2 * TILE
        mine = mine_ref[:, start : start + span, :].reshape(chips * span, width)
        other = other_ref[:, start : start + span, :].reshape(chips * span, width)
        own_rows = pl.ds(pl.multiple_of(leaf * leaf_len, leaf_len), leaf_len)
        keys = jnp.concatenate([mine, other, own_ref[own_rows, :]], 0)
        paged = 2 * chips * span
        grads = jnp.concatenate([grad_ref[leaf], theirs_ref[at, :, :latent]], 0)
        stacked = jnp.concatenate(
            [query_ref[leaf], theirs_ref[at, :, latent : latent + width], jnp.concatenate([grads, blank], 1)], 0
        )
        products = dot(keys, stacked, (1, 1))
        key_at = iota((paged + leaf_len, 2 * rows), 0)
        token_at = iota((paged + leaf_len, 2 * rows), 1) % rows // (rows // leaf_len)
        strange = 0 if at < 2 else jnp.abs(key_at % tail // page_rows - (at - 2))
        gap = jnp.where(key_at < paged, strange, jnp.maximum(key_at - paged - token_at, 0))
        scores = jnp.where(gap == 0, softmax_scale * products[:, : 2 * rows], -jnp.inf)
        grad_weights = products[:, 2 * rows :]
        raised = jnp.exp(scores - jnp.max(scores, 0, keepdims=True))
        weights = raised / jnp.sum(raised, 0, keepdims=True)
        row_delta = jnp.sum(weights * grad_weights, 0, keepdims=True)
        dscore = softmax_scale * (weights * (grad_weights - row_delta))
        left = jnp.concatenate([dscore.astype(BF16), weights.astype(BF16)], 1)
        key_grads = dot(left, stacked, (1, 0))
        if at < 2:
            out_mine[:, start : start + span, :] = (
                key_grads[: chips * span].astype(BF16).reshape(chips, span, width)
            )
            out_other[:, start : start + span, :] = (
                key_grads[chips * span : paged].astype(BF16).reshape(chips, span, width)
            )
        else:
            small = key_grads[:paged] if small is None else small + key_grads[:paged]
        leaf_tails.append((leaf, key_grads[paged : paged + half], key_grads[paged + half :]))
    first = core_ref[0] == 0
    for chip in range(chips):
        low = high = jnp.zeros((half, width), F32)
        for leaf, leaf_low, leaf_high in leaf_tails:
            low = low + jnp.where(leaf == chip, leaf_low, 0.0)
            high = high + jnp.where(leaf == chip, leaf_high, 0.0)
        for out, part, rest in (
            (out_mine, small[: chips * tail], jnp.where(first, low, high)),
            (out_other, small[chips * tail :], jnp.where(first, high, low)),
        ):
            end = jnp.concatenate([part[chip * tail : (chip + 1) * tail], rest], 0)
            out[chip, 2 * TILE : 2 * TILE + tail + half, :] = end.astype(BF16)


def collect_kernel(row_local, slot_ref, parts_ref, out_ref, leaf_ref):
    chips, part_rows, width = parts_ref.shape
    set_rows = part_rows - leaf_ref.shape[0]
    sums = []
    for parity in range(2):
        total = parts_ref[parity].astype(F32)
        for chip in range(parity + 2, chips, 2):
            total = total + parts_ref[chip].astype(F32)
        sums.append(total)
    leaf_ref[...] = sums[0][set_rows:] + sums[1][set_rows:]
    requests = jnp.concatenate([sums[0][:set_rows], sums[1][:set_rows]], 0).astype(BF16)
    gather = gather_of(slot_ref, row_local, out_ref.shape[0])
    out_ref[...] = dot(gather, requests, (0, 0)).astype(BF16)


def return_kernel(row_local, low_ref, incoming_ref, neighbour_ref, arrived_ref, out_ref):
    slot_rows = arrived_ref.shape[0]
    column = iota((1, slot_rows), 1)
    per_home = CAPACITY * row_local
    low = low_ref[0]
    pages = []
    for ref in (incoming_ref, neighbour_ref):
        asked = asked_of(ref[...], slot_rows, row_local)
        asked = jnp.where(low == 0, asked[:CAPACITY], asked[CAPACITY:])
        pages.append(jnp.where(column // row_local % CAPACITY == 0, asked[:1], asked[1:]))
    page = jnp.where(column // per_home % 2 == low, pages[0], pages[1])
    wanted_row = jnp.where(page > 0, (page - 1) * row_local + column % row_local, -1)
    lookup = (iota((out_ref.shape[0], slot_rows), 0) == wanted_row).astype(BF16)
    out_ref[...] = dot(lookup, arrived_ref[...], (1, 0))


def call(kernel, name, out_shape, in_specs, out_specs, scratch=()):
    return pl.pallas_call(
        kernel, name=name, out_shape=out_shape, in_specs=in_specs, out_specs=out_specs,
        scratch_shapes=list(scratch), compiler_params=PARAMS,
    )


def on_device(
    queries, leaf_kv, grad_out, latent_pages, ancestor_home, ancestor_page, ancestor_count
):
    pair_count = lax.axis_size("z") * lax.axis_size("xh")
    home_count = 2 * pair_count
    low = lax.axis_index("xl").astype(jnp.int32).reshape(1)
    chips = lax.axis_size("y")
    parity = (lax.axis_index("y") % 2).astype(jnp.int32).reshape(1)
    core = lax.axis_index("core").astype(jnp.int32).reshape(1)
    tok_rows, head_local, width = queries.shape
    latent = grad_out.shape[2]
    leaf_count, anc_slots = ancestor_home.shape
    leaf_len = tok_rows // leaf_count
    page_local, row_local = latent_pages.shape[:2]
    live_count = leaf_count // 2 * (anc_slots + 1)
    set_rows = live_count // 2 * row_local
    slot_rows = home_count * CAPACITY * row_local
    block_rows = leaf_len * head_local
    pair_width = -(-(latent + width) // 128) * 128
    swap = [(0, 1), (1, 0)]
    neighbours = [(i, i ^ 1) for i in range(chips)]
    shape = jax.ShapeDtypeStruct

    with jax.named_scope("plan"):
        half = leaf_count // 2
        kept, given, slots, wanted = pl.pallas_call(
            plan_kernel,
            name="plan",
            in_specs=[SMEM] + [pl.BlockSpec(memory_space=pl.ANY)] * 3,
            out_specs=[SMEM, SMEM, SMEM, VMEM],
            out_shape=[
                shape((half + 1,), jnp.int32),
                shape((half + 1,), jnp.int32),
                shape((live_count + 1,), jnp.int32),
                shape((pair_count, 2 * CAPACITY), jnp.int32),
            ],
            scratch_shapes=[
                pltpu.SMEM((home_count,), jnp.int32),
                pltpu.SMEM((anc_slots, leaf_count), jnp.int32),
                pltpu.SMEM((anc_slots, leaf_count), jnp.int32),
                pltpu.SMEM((leaf_count,), jnp.int32),
                pltpu.SemaphoreType.DMA((3,)),
            ],
            compiler_params=pltpu.CompilerParams(vmem_limit_bytes=56 * 1024 * 1024),
        )(parity, ancestor_home.T, ancestor_page.T, ancestor_count)

    with jax.named_scope("offsets"):
        incoming = lax.all_to_all(wanted, PAIRS, split_axis=0, concat_axis=0, tiled=True)
        neighbour_incoming = lax.ppermute(incoming, "xl", swap)

    with jax.named_scope("pair"):
        leaf_queries = queries.reshape(leaf_count, block_rows, width)
        leaf_grad_out = grad_out.reshape(leaf_count, block_rows, latent)
        leaving = pl.pallas_call(
            pick_kernel,
            grid_spec=pltpu.PrefetchScalarGridSpec(
                num_scalar_prefetch=1,
                grid=(half,),
                in_specs=[
                    pl.BlockSpec((1, block_rows, width), lambda i, o: (o[i], 0, 0)),
                    pl.BlockSpec((1, block_rows, latent), lambda i, o: (o[i], 0, 0)),
                ],
                out_specs=pl.BlockSpec((1, block_rows, pair_width), lambda i, o: (i, 0, 0)),
            ),
            out_shape=shape((half, block_rows, pair_width), BF16),
            compiler_params=PARAMS,
            name="pick",
        )(given, leaf_queries, leaf_grad_out)
        neighbour_pages = lax.ppermute(latent_pages, "xl", swap)
        pages = latent_pages.reshape(page_local * row_local, width)
        pages, leaving = lax.optimization_barrier((pages, leaving))
        theirs = lax.ppermute(leaving, "y", neighbours)

    with jax.named_scope("fetch"):
        served = call(
            lambda *refs: serve_kernel(row_local, *refs), "serve",
            shape((pair_count, 2 * CAPACITY * row_local, width), BF16),
            [SMEM, VMEM, VMEM, VMEM], VMEM,
        )(low, incoming, pages, neighbour_pages.reshape(page_local * row_local, width))
        returned = lax.all_to_all(served, PAIRS, split_axis=0, concat_axis=0, tiled=True)
        leaving_pages = call(
            lambda *refs: compact_kernel(row_local, *refs), "compact",
            shape((chips, set_rows, width), BF16), [SMEM, VMEM], VMEM,
        )(slots, returned.reshape(slot_rows, width))

    with jax.named_scope("spread"):
        mine = lax.all_to_all(leaving_pages, "y", split_axis=0, concat_axis=0, tiled=True)
        other = lax.ppermute(mine, "core", swap)

    with jax.named_scope("attend"):
        part_shape = shape((chips, set_rows + leaf_len // 2, width), BF16)
        part_mine, part_other = call(
            attention_kernel, "attention", [part_shape] * 2, [SMEM] * 2 + [VMEM] * 6, [VMEM] * 2
        )(kept, core, leaf_queries, leaf_grad_out, theirs, mine, other, leaf_kv)

    with jax.named_scope("collect"):
        from_core = lax.ppermute(part_other, "core", swap)
        both = (part_mine.astype(F32) + from_core.astype(F32)).astype(BF16)
        parts = lax.all_to_all(both, "y", split_axis=0, concat_axis=0, tiled=True)
        outbound, leaf_grads = call(
            lambda *refs: collect_kernel(row_local, *refs), "collect",
            [shape((slot_rows, width), BF16), shape((leaf_len // 2, width), F32)],
            [SMEM, VMEM], [VMEM, VMEM],
        )(slots, parts)

    with jax.named_scope("home"):
        arrived = lax.all_to_all(
            outbound.reshape(home_count, CAPACITY * row_local, width),
            HOME, split_axis=0, concat_axis=0, tiled=True,
        )
        page_grads = call(
            lambda *refs: return_kernel(row_local, *refs), "return",
            shape((page_local * row_local, width), F32), [SMEM, VMEM, VMEM, VMEM], VMEM,
        )(low, incoming, neighbour_incoming, arrived.reshape(slot_rows, width))
    return (page_grads.reshape(page_local, row_local, width), leaf_grads)


def solution(mesh):
    home_count, head_count = mesh.devices.shape
    side = math.isqrt(home_count)
    split = Mesh(
        mesh.devices.reshape(side, home_count // side // 2, 2, head_count // 2, 2),
        HOME + ("y", "core"),
    )
    head = ("y", "core")
    placed = (
        P(HOME, head, None),
        P(HOME, None),
        P(HOME, head, None),
        P(HOME, head, None),
        P(HOME, None),
        P(HOME, None),
        P(HOME),
    )
    return jax.shard_map(
        on_device,
        mesh=split,
        in_specs=placed,
        out_specs=(P(HOME, head, None), P(HOME + head, None)),
        check_vma=False,
    )
```

```python
import math

import jax
import jax.numpy as jnp
from jax import lax
from jax.experimental import pallas as pl
from jax.experimental.pallas import tpu as pltpu
from jax.sharding import Mesh
from jax.sharding import PartitionSpec as P

softmax_scale = 192.0 ** (-0.5)
BF16 = jnp.bfloat16
F32 = jnp.float32
HOME = ("z", "x")
CAPACITY = 2
TILE = 16
VMEM = pl.BlockSpec(memory_space=pltpu.VMEM)
SMEM = pl.BlockSpec(memory_space=pltpu.SMEM)
PARAMS = pltpu.CompilerParams(vmem_limit_bytes=32 * 1024 * 1024)


def iota(shape, dim):
    return lax.broadcasted_iota(jnp.int32, shape, dim)


def dot(a, b, contract):
    return lax.dot_general(a, b, ((contract[:1], contract[1:]), ((), ())), preferred_element_type=F32)


def plan_kernel(
    parity_ref, home_hbm, page_hbm, count_hbm, kept_ref, given_ref, slot_ref, wanted_ref, seen,
    home_ref, page_ref, count_ref, sems,
):
    copies = [
        pltpu.make_async_copy(source, target, sems.at[at])
        for at, (source, target) in enumerate(
            ((home_hbm, home_ref), (page_hbm, page_ref), (count_hbm, count_ref))
        )
    ]
    for copy in copies:
        copy.start()
    for home in range(seen.shape[0]):
        seen[home] = 0
    for copy in copies:
        copy.wait()
    anc_slots, leaf_count = home_ref.shape
    set_size = 2 * anc_slots + 2
    live_count = slot_ref.shape[0] - 1
    spare = kept_ref.shape[0] - 1
    row, column = iota(wanted_ref.shape, 0), iota(wanted_ref.shape, 1)
    wanted = jnp.zeros(wanted_ref.shape, jnp.int32)
    big_seen = small_seen = jnp.int32(0)
    for leaf in range(leaf_count):
        count = count_ref[leaf]
        big = jnp.where(count > 1, 1, 0)
        set_at = jnp.where(big == 1, big_seen // 2, small_seen // 2)
        place = jnp.where(big == 1, big_seen % 2, 2 + small_seen % 2)
        keep = set_at == parity_ref[0]
        kept_ref[jnp.where(keep, place, spare)] = leaf
        given_ref[jnp.where(keep, spare, place)] = leaf
        first = set_at * set_size + jnp.where(
            big == 1, place * anc_slots, 2 * anc_slots + small_seen % 2
        )
        for slot in range(anc_slots):
            live = jnp.where(slot < count, 1, 0)
            home = home_ref[slot, leaf]
            rank = seen[home]
            seen[home] = rank + live
            slot_ref[jnp.where(live == 1, first + slot, live_count)] = home * CAPACITY + rank
            value = page_ref[slot, leaf] + 1
            at = jnp.where(live == 1, home * CAPACITY + rank, -1)
            wanted = jnp.where(row * CAPACITY + column == at, value, wanted)
        big_seen += big
        small_seen += 1 - big
    wanted_ref[...] = wanted


def lookup_of(incoming, row_local, page_rows):
    home_count = incoming.shape[0]
    slot_rows = home_count * CAPACITY * row_local
    per_home = CAPACITY * row_local
    spread = (iota((home_count, slot_rows), 1) // per_home == iota((home_count, slot_rows), 0)).astype(BF16)
    asked = dot(incoming.astype(F32).astype(BF16), spread, (0, 0)).astype(jnp.int32)
    column = iota((1, slot_rows), 1)
    asked = jnp.where((column % per_home) // row_local == 0, asked[:1], asked[1:])
    wanted_row = jnp.where(asked > 0, (asked - 1) * row_local + column % row_local, -1)
    return (iota((page_rows, slot_rows), 0) == wanted_row).astype(BF16)


def serve_kernel(row_local, incoming_ref, pages_ref, out_ref):
    lookup = lookup_of(incoming_ref[...], row_local, pages_ref.shape[0])
    out_ref[...] = dot(lookup, pages_ref[...], (0, 0)).astype(BF16).reshape(out_ref.shape)


def gather_of(slot_ref, row_local, slot_rows):
    live_count = slot_ref.shape[0] - 1
    shape = (live_count * row_local, slot_rows)
    row = iota((shape[0], 1), 0)
    target = jnp.zeros((shape[0], 1), jnp.int32)
    for at in range(live_count):
        target = jnp.where(row // row_local == at, slot_ref[at] * row_local, target)
    return (iota(shape, 1) == target + row % row_local).astype(BF16)


def compact_kernel(row_local, slot_ref, returned_ref, out_ref):
    slot_rows, width = returned_ref.shape
    chips, set_rows, _ = out_ref.shape
    fetched = dot(gather_of(slot_ref, row_local, slot_rows), returned_ref[...], (1, 0))
    sets = [fetched[:set_rows].astype(BF16), fetched[set_rows:].astype(BF16)]
    for chip in range(chips):
        out_ref[chip] = sets[chip % 2]


def pick_kernel(order_ref, query_ref, grad_ref, out_ref):
    latent, width = grad_ref.shape[2], query_ref.shape[2]
    out_ref[0, :, :latent] = grad_ref[0]
    blank = jnp.zeros((out_ref.shape[1], out_ref.shape[2] - latent - width), BF16)
    out_ref[0, :, latent:] = jnp.concatenate([query_ref[0], blank], 1)


def keys_of(mine_ref, at):
    chips, set_rows, width = mine_ref.shape
    tail = set_rows - 2 * TILE
    span = TILE if at < 2 else tail
    start = at * TILE if at < 2 else 2 * TILE
    return mine_ref[:, start : start + span, :].reshape(chips * span, width)


def stacked_of(block_refs, at, latent, width):
    queries = [ref[at, :, latent : latent + width] for ref in block_refs]
    grads = [ref[at, :, :latent] for ref in block_refs]
    blank = jnp.zeros((len(grads) * grads[0].shape[0], width - latent), BF16)
    return jnp.concatenate(queries + [jnp.concatenate([jnp.concatenate(grads, 0), blank], 1)], 0)


def scores_kernel(
    latent, leaf_len, order_ref, core_ref, mine_ref, own_ref, b0_ref, b1_ref, b2_ref, b3_ref,
    big_raised, big_grad, small_raised, small_grad, stats_ref,
):
    width = mine_ref.shape[2]
    block_refs = (b0_ref, b1_ref, b2_ref, b3_ref)
    block_rows = b0_ref.shape[1]
    rows = len(block_refs) * block_rows
    half = leaf_len // 2
    tail = mine_ref.shape[1] - 2 * TILE
    page_rows = TILE // 4
    for at in range(4):
        own_rows = pl.ds(pl.multiple_of(order_ref[at] * leaf_len, leaf_len), leaf_len)
        own = own_ref[own_rows, :].astype(F32)
        own = jnp.where(core_ref[0] == 0, own[:half], own[half:]).astype(BF16)
        pages = keys_of(mine_ref, at)
        paged = pages.shape[0]
        keys = jnp.concatenate([pages, own], 0)
        products = dot(keys, stacked_of(block_refs, at, latent, width), (1, 1))
        key_at = iota((paged + half, rows), 0)
        token_at = iota((paged + half, rows), 1) % block_rows // (block_rows // leaf_len)
        strange = 0 if at < 2 else jnp.abs(key_at % tail // page_rows - (at - 2))
        late = jnp.maximum(key_at - paged + half * core_ref[0] - token_at, 0)
        gap = jnp.where(key_at < paged, strange, late)
        scores = jnp.where(gap == 0, softmax_scale * products[:, :rows], -jnp.inf)
        grad_weights = products[:, rows:]
        top = jnp.max(scores, 0, keepdims=True)
        raised = jnp.exp(scores - top)
        total = jnp.sum(raised, 0, keepdims=True)
        weighted = jnp.sum(raised * grad_weights, 0, keepdims=True)
        stats_ref[at] = jnp.concatenate([top, total, weighted, jnp.zeros((5, rows), F32)], 0)
        raised_ref, grad_ref = (big_raised, big_grad) if at < 2 else (small_raised, small_grad)
        raised_ref[at % 2] = raised
        grad_ref[at % 2] = grad_weights


def grads_kernel(
    latent, leaf_len, order_ref, mine_stats, other_stats, b0_ref, b1_ref, b2_ref, b3_ref,
    big_raised, big_grad, small_raised, small_grad, out_ref,
):
    chips, _, width = out_ref.shape
    block_refs = (b0_ref, b1_ref, b2_ref, b3_ref)
    block_rows = b0_ref.shape[1]
    half = leaf_len // 2
    small = None
    leaf_parts = []

    def swapped(at):
        cut = [other_stats[at, :, i * block_rows : (i + 1) * block_rows] for i in (1, 0, 3, 2)]
        return jnp.concatenate(cut, 1)

    for at in range(4):
        there = swapped(at)
        top, top_other = mine_stats[at, 0:1, :], there[0:1]
        most = jnp.maximum(top, top_other)
        factor, factor_other = jnp.exp(top - most), jnp.exp(top_other - most)
        total = factor * mine_stats[at, 1:2, :] + factor_other * there[1:2]
        weighted = factor * mine_stats[at, 2:3, :] + factor_other * there[2:3]
        row_delta = weighted / total
        raised_ref, grad_ref = (big_raised, big_grad) if at < 2 else (small_raised, small_grad)
        weights = raised_ref[at % 2] * (factor / total)
        dscore = softmax_scale * (weights * (grad_ref[at % 2] - row_delta))
        left = jnp.concatenate([dscore.astype(BF16), weights.astype(BF16)], 1)
        key_grads = dot(left, stacked_of(block_refs, at, latent, width), (1, 0))
        paged = key_grads.shape[0] - half
        if at < 2:
            out_ref[:, at * TILE : (at + 1) * TILE, :] = (
                key_grads[:paged].astype(BF16).reshape(chips, TILE, width)
            )
        else:
            small = key_grads[:paged] if small is None else small + key_grads[:paged]
        leaf_parts.append((order_ref[at], key_grads[paged:]))
    tail = small.shape[0] // chips
    for chip in range(chips):
        own = jnp.zeros((half, width), F32)
        for leaf, part in leaf_parts:
            own = own + jnp.where(leaf == chip, part, 0.0)
        end = jnp.concatenate([small[chip * tail : (chip + 1) * tail], own], 0)
        out_ref[chip, 2 * TILE : 2 * TILE + tail + half, :] = end.astype(BF16)


def collect_kernel(row_local, slot_ref, parts_ref, out_ref, leaf_ref):
    chips, part_rows, width = parts_ref.shape
    set_rows = part_rows - leaf_ref.shape[0]
    sums = []
    for parity in range(2):
        total = parts_ref[parity].astype(F32)
        for chip in range(parity + 2, chips, 2):
            total = total + parts_ref[chip].astype(F32)
        sums.append(total)
    leaf_ref[...] = sums[0][set_rows:] + sums[1][set_rows:]
    requests = jnp.concatenate([sums[0][:set_rows], sums[1][:set_rows]], 0).astype(BF16)
    gather = gather_of(slot_ref, row_local, out_ref.shape[0])
    out_ref[...] = dot(gather, requests, (0, 0)).astype(BF16)


def return_kernel(row_local, incoming_ref, arrived_ref, out_ref):
    lookup = lookup_of(incoming_ref[...], row_local, out_ref.shape[0] * row_local)
    out_ref[...] = dot(lookup, arrived_ref[...], (1, 0)).reshape(out_ref.shape)


def call(kernel, name, out_shape, in_specs, out_specs, scratch=()):
    return pl.pallas_call(
        kernel, name=name, out_shape=out_shape, in_specs=in_specs, out_specs=out_specs,
        scratch_shapes=list(scratch), compiler_params=PARAMS,
    )


def on_device(
    queries, leaf_kv, grad_out, latent_pages, ancestor_home, ancestor_page, ancestor_count
):
    home_count = lax.axis_size("z") * lax.axis_size("x")
    chips = lax.axis_size("y")
    parity = (lax.axis_index("y") % 2).astype(jnp.int32).reshape(1)
    core = lax.axis_index("core").astype(jnp.int32).reshape(1)
    tok_rows, head_local, width = queries.shape
    latent = grad_out.shape[2]
    leaf_count, anc_slots = ancestor_home.shape
    leaf_len = tok_rows // leaf_count
    page_local, row_local = latent_pages.shape[:2]
    live_count = leaf_count // 2 * (anc_slots + 1)
    set_rows = live_count // 2 * row_local
    slot_rows = home_count * CAPACITY * row_local
    block_rows = leaf_len * head_local
    pair_width = -(-(latent + width) // 128) * 128
    swap = [(0, 1), (1, 0)]
    neighbours = [(i, i ^ 1) for i in range(chips)]
    shape = jax.ShapeDtypeStruct

    with jax.named_scope("plan"):
        half = leaf_count // 2
        kept, given, slots, wanted = pl.pallas_call(
            plan_kernel,
            name="plan",
            in_specs=[SMEM] + [pl.BlockSpec(memory_space=pl.ANY)] * 3,
            out_specs=[SMEM, SMEM, SMEM, VMEM],
            out_shape=[
                shape((half + 1,), jnp.int32),
                shape((half + 1,), jnp.int32),
                shape((live_count + 1,), jnp.int32),
                shape((home_count, CAPACITY), jnp.int32),
            ],
            scratch_shapes=[
                pltpu.SMEM((home_count,), jnp.int32),
                pltpu.SMEM((anc_slots, leaf_count), jnp.int32),
                pltpu.SMEM((anc_slots, leaf_count), jnp.int32),
                pltpu.SMEM((leaf_count,), jnp.int32),
                pltpu.SemaphoreType.DMA((3,)),
            ],
            compiler_params=pltpu.CompilerParams(vmem_limit_bytes=56 * 1024 * 1024),
        )(parity, ancestor_home.T, ancestor_page.T, ancestor_count)

    with jax.named_scope("offsets"):
        incoming = lax.all_to_all(wanted, HOME, split_axis=0, concat_axis=0, tiled=True)

    with jax.named_scope("pair"):
        leaf_queries = queries.reshape(leaf_count, block_rows, width)
        leaf_grad_out = grad_out.reshape(leaf_count, block_rows, latent)
        def pick(leaves, name):
            return pl.pallas_call(
                pick_kernel,
                grid_spec=pltpu.PrefetchScalarGridSpec(
                    num_scalar_prefetch=1,
                    grid=(half,),
                    in_specs=[
                        pl.BlockSpec((1, block_rows, width), lambda i, o: (o[i], 0, 0)),
                        pl.BlockSpec((1, block_rows, latent), lambda i, o: (o[i], 0, 0)),
                    ],
                    out_specs=pl.BlockSpec((1, block_rows, pair_width), lambda i, o: (i, 0, 0)),
                ),
                out_shape=shape((half, block_rows, pair_width), BF16),
                compiler_params=PARAMS,
                name=name,
            )(leaves, leaf_queries, leaf_grad_out)

        leaving = pick(given, "pick_given")
        pages = latent_pages.reshape(page_local * row_local, width)
        pages, leaving = lax.optimization_barrier((pages, leaving))
        theirs = lax.ppermute(
            lax.optimization_barrier((leaving, incoming))[0], "y", neighbours
        )
        ours = pick(kept, "pick_kept")
        blocks = [ours, lax.ppermute(ours, "core", swap), theirs, lax.ppermute(theirs, "core", swap)]

    with jax.named_scope("fetch"):
        served = call(
            lambda *refs: serve_kernel(row_local, *refs), "serve",
            shape((home_count, CAPACITY * row_local, width), BF16), [VMEM, VMEM], VMEM,
        )(incoming, pages)
        returned = lax.all_to_all(served, HOME, split_axis=0, concat_axis=0, tiled=True)
        leaving_pages = call(
            lambda *refs: compact_kernel(row_local, *refs), "compact",
            shape((chips, set_rows, width), BF16), [SMEM, VMEM], VMEM,
        )(slots, returned.reshape(slot_rows, width))

    with jax.named_scope("spread"):
        mine = lax.all_to_all(leaving_pages, "y", split_axis=0, concat_axis=0, tiled=True)

    with jax.named_scope("attend"):
        rows = 4 * block_rows
        tail = set_rows - 2 * TILE
        big_shape = shape((2, chips * TILE + leaf_len // 2, rows), F32)
        small_shape = shape((2, chips * tail + leaf_len // 2, rows), F32)
        *partial, stats = call(
            lambda *refs: scores_kernel(latent, leaf_len, *refs), "scores",
            [big_shape, big_shape, small_shape, small_shape, shape((4, 8, rows), F32)],
            [SMEM] * 2 + [VMEM] * 6, [VMEM] * 5,
        )(kept, core, mine, leaf_kv, *blocks)
        other_stats = lax.ppermute(stats, "core", swap)
        part = call(
            lambda *refs: grads_kernel(latent, leaf_len, *refs), "grads",
            shape((chips, set_rows + leaf_len // 2, width), BF16), [SMEM] + [VMEM] * 10, VMEM,
        )(kept, stats, other_stats, *blocks, *partial)

    with jax.named_scope("collect"):
        parts = lax.all_to_all(part, "y", split_axis=0, concat_axis=0, tiled=True)
        outbound, leaf_grads = call(
            lambda *refs: collect_kernel(row_local, *refs), "collect",
            [shape((slot_rows, width), BF16), shape((leaf_len // 2, width), F32)],
            [SMEM, VMEM], [VMEM, VMEM],
        )(slots, parts)

    with jax.named_scope("home"):
        arrived = lax.all_to_all(
            outbound.reshape(home_count, CAPACITY * row_local, width),
            HOME, split_axis=0, concat_axis=0, tiled=True,
        )
        page_grads = call(
            lambda *refs: return_kernel(row_local, *refs), "return",
            shape((page_local, row_local, width), F32), [VMEM, VMEM], VMEM,
        )(incoming, arrived.reshape(slot_rows, width))
    return page_grads, leaf_grads


def solution(mesh):
    home_count, head_count = mesh.devices.shape
    side = math.isqrt(home_count)
    split = Mesh(
        mesh.devices.reshape(side, home_count // side, head_count // 2, 2), ("z", "x", "y", "core")
    )
    head = ("y", "core")
    placed = (
        P(HOME, head, None),
        P(HOME, None),
        P(HOME, head, None),
        P(HOME, head, None),
        P(HOME, None),
        P(HOME, None),
        P(HOME),
    )
    return jax.shard_map(
        on_device,
        mesh=split,
        in_specs=placed,
        out_specs=(P(HOME, head, None), P(HOME + head, None)),
        check_vma=False,
    )
```

```python
import math

import jax
import jax.numpy as jnp
from jax import lax
from jax.experimental import pallas as pl
from jax.experimental.pallas import tpu as pltpu
from jax.sharding import Mesh
from jax.sharding import PartitionSpec as P

softmax_scale = 192.0 ** (-0.5)
BF16 = jnp.bfloat16
F32 = jnp.float32
HOME = ("z", "x")
CAPACITY = 2
TILE = 16
VMEM = pl.BlockSpec(memory_space=pltpu.VMEM)
SMEM = pl.BlockSpec(memory_space=pltpu.SMEM)
PARAMS = pltpu.CompilerParams(vmem_limit_bytes=32 * 1024 * 1024)


def iota(shape, dim):
    return lax.broadcasted_iota(jnp.int32, shape, dim)


def dot(a, b, contract):
    return lax.dot_general(a, b, ((contract[:1], contract[1:]), ((), ())), preferred_element_type=F32)


def plan_kernel(
    parity_ref, home_hbm, page_hbm, count_hbm, kept_ref, given_ref, slot_ref, wanted_ref, seen,
    home_ref, page_ref, count_ref, sems,
):
    copies = [
        pltpu.make_async_copy(source, target, sems.at[at])
        for at, (source, target) in enumerate(
            ((home_hbm, home_ref), (page_hbm, page_ref), (count_hbm, count_ref))
        )
    ]
    for copy in copies:
        copy.start()
    for home in range(seen.shape[0]):
        seen[home] = 0
    for copy in copies:
        copy.wait()
    anc_slots, leaf_count = home_ref.shape
    set_size = 2 * anc_slots + 2
    live_count = slot_ref.shape[0] - 1
    spare = kept_ref.shape[0] - 1
    row, column = iota(wanted_ref.shape, 0), iota(wanted_ref.shape, 1)
    wanted = jnp.zeros(wanted_ref.shape, jnp.int32)
    big_seen = small_seen = jnp.int32(0)
    for leaf in range(leaf_count):
        count = count_ref[leaf]
        big = jnp.where(count > 1, 1, 0)
        set_at = jnp.where(big == 1, big_seen // 2, small_seen // 2)
        place = jnp.where(big == 1, big_seen % 2, 2 + small_seen % 2)
        keep = set_at == parity_ref[0]
        kept_ref[jnp.where(keep, place, spare)] = leaf
        given_ref[jnp.where(keep, spare, place)] = leaf
        first = set_at * set_size + jnp.where(
            big == 1, place * anc_slots, 2 * anc_slots + small_seen % 2
        )
        for slot in range(anc_slots):
            live = jnp.where(slot < count, 1, 0)
            home = home_ref[slot, leaf]
            rank = seen[home]
            seen[home] = rank + live
            slot_ref[jnp.where(live == 1, first + slot, live_count)] = home * CAPACITY + rank
            value = page_ref[slot, leaf] + 1
            at = jnp.where(live == 1, home * CAPACITY + rank, -1)
            wanted = jnp.where(row * CAPACITY + column == at, value, wanted)
        big_seen += big
        small_seen += 1 - big
    wanted_ref[...] = wanted


def lookup_of(incoming, row_local, page_rows):
    home_count = incoming.shape[0]
    slot_rows = home_count * CAPACITY * row_local
    per_home = CAPACITY * row_local
    spread = (iota((home_count, slot_rows), 1) // per_home == iota((home_count, slot_rows), 0)).astype(BF16)
    asked = dot(incoming.astype(F32).astype(BF16), spread, (0, 0)).astype(jnp.int32)
    column = iota((1, slot_rows), 1)
    asked = jnp.where((column % per_home) // row_local == 0, asked[:1], asked[1:])
    wanted_row = jnp.where(asked > 0, (asked - 1) * row_local + column % row_local, -1)
    return (iota((page_rows, slot_rows), 0) == wanted_row).astype(BF16)


def serve_kernel(row_local, incoming_ref, pages_ref, out_ref):
    lookup = lookup_of(incoming_ref[...], row_local, pages_ref.shape[0])
    out_ref[...] = dot(lookup, pages_ref[...], (0, 0)).astype(BF16).reshape(out_ref.shape)


def gather_of(slot_ref, row_local, slot_rows):
    live_count = slot_ref.shape[0] - 1
    shape = (live_count * row_local, slot_rows)
    row = iota((shape[0], 1), 0)
    target = jnp.zeros((shape[0], 1), jnp.int32)
    for at in range(live_count):
        target = jnp.where(row // row_local == at, slot_ref[at] * row_local, target)
    return (iota(shape, 1) == target + row % row_local).astype(BF16)


def compact_kernel(row_local, slot_ref, returned_ref, out_ref):
    slot_rows, width = returned_ref.shape
    chips, set_rows, _ = out_ref.shape
    fetched = dot(gather_of(slot_ref, row_local, slot_rows), returned_ref[...], (1, 0))
    sets = [fetched[:set_rows].astype(BF16), fetched[set_rows:].astype(BF16)]
    for chip in range(chips):
        out_ref[chip] = sets[chip % 2]


def pick_kernel(order_ref, query_ref, grad_ref, out_ref):
    latent, width = grad_ref.shape[2], query_ref.shape[2]
    out_ref[0, :, :latent] = grad_ref[0]
    blank = jnp.zeros((out_ref.shape[1], out_ref.shape[2] - latent - width), BF16)
    out_ref[0, :, latent:] = jnp.concatenate([query_ref[0], blank], 1)


def stacked_of(block_refs, latent, width):
    queries = [ref[0, :, latent : latent + width] for ref in block_refs]
    grads = [ref[0, :, :latent] for ref in block_refs]
    blank = jnp.zeros((len(grads) * grads[0].shape[0], width - latent), BF16)
    return jnp.concatenate(queries + [jnp.concatenate([jnp.concatenate(grads, 0), blank], 1)], 0)


def scores_kernel(
    latent, order_ref, core_ref, mine_ref, own_ref, b0_ref, b1_ref, b2_ref, b3_ref,
    raised_ref, grad_ref, stats_ref,
):
    at = pl.program_id(0)
    chips, set_rows, width = mine_ref.shape
    block_refs = (b0_ref, b1_ref, b2_ref, b3_ref)
    block_rows = b0_ref.shape[1]
    rows = len(block_refs) * block_rows
    leaf_len = own_ref.shape[0]
    half = leaf_len // 2
    tail = set_rows - 2 * TILE

    def work(big):
        span = TILE if big else tail
        start = pl.multiple_of(at * TILE, TILE) if big else 2 * TILE
        pages = mine_ref[:, pl.ds(start, span), :].reshape(chips * span, width)
        paged = chips * span
        own = own_ref[...].astype(F32)
        own = jnp.where(core_ref[0] == 0, own[:half], own[half:]).astype(BF16)
        keys = jnp.concatenate([pages, own], 0)
        products = dot(keys, stacked_of(block_refs, latent, width), (1, 1))
        key_at = iota((paged + half, rows), 0)
        token_at = iota((paged + half, rows), 1) % block_rows // (block_rows // leaf_len)
        strange = 0 if big else jnp.abs(key_at % tail // (TILE // 4) - (at - 2))
        late = jnp.maximum(key_at - paged + half * core_ref[0] - token_at, 0)
        gap = jnp.where(key_at < paged, strange, late)
        scores = jnp.where(gap == 0, softmax_scale * products[:, :rows], -jnp.inf)
        grad_weights = products[:, rows:]
        top = jnp.max(scores, 0, keepdims=True)
        raised = jnp.exp(scores - top)
        total = jnp.sum(raised, 0, keepdims=True)
        weighted = jnp.sum(raised * grad_weights, 0, keepdims=True)
        stats_ref[0] = jnp.concatenate([top, total, weighted, jnp.zeros((5, rows), F32)], 0)
        raised_ref[0, : paged + half, :] = raised
        grad_ref[0, : paged + half, :] = grad_weights

    pl.when(at < 2)(lambda: work(True))
    pl.when(at >= 2)(lambda: work(False))


def grads_kernel(
    latent, order_ref, mine_stats, other_stats, b0_ref, b1_ref, b2_ref, b3_ref,
    raised_ref, grad_ref, out_ref, small_ref, leaf_ref,
):
    at = pl.program_id(0)
    chips, part_rows, width = out_ref.shape
    block_refs = (b0_ref, b1_ref, b2_ref, b3_ref)
    block_rows = b0_ref.shape[1]
    half = leaf_ref.shape[1]
    tail = part_rows - half - 2 * TILE

    def work(big):
        keys = chips * (TILE if big else tail) + half
        cut = [other_stats[0, :, i * block_rows : (i + 1) * block_rows] for i in (1, 0, 3, 2)]
        there = jnp.concatenate(cut, 1)
        top, top_there = mine_stats[0, 0:1, :], there[0:1]
        most = jnp.maximum(top, top_there)
        factor, factor_there = jnp.exp(top - most), jnp.exp(top_there - most)
        total = factor * mine_stats[0, 1:2, :] + factor_there * there[1:2]
        row_delta = (factor * mine_stats[0, 2:3, :] + factor_there * there[2:3]) / total
        weights = raised_ref[0, :keys, :] * (factor / total)
        dscore = softmax_scale * (weights * (grad_ref[0, :keys, :] - row_delta))
        left = jnp.concatenate([dscore.astype(BF16), weights.astype(BF16)], 1)
        key_grads = dot(left, stacked_of(block_refs, latent, width), (1, 0))
        paged = keys - half
        if big:
            spot = pl.ds(pl.multiple_of(at * TILE, TILE), TILE)
            out_ref[:, spot, :] = key_grads[:paged].astype(BF16).reshape(chips, TILE, width)
        else:
            small_ref[...] += key_grads[:paged]
        leaf_ref[order_ref[at]] = key_grads[paged:]

    @pl.when(at == 0)
    def _():
        small_ref[...] = jnp.zeros(small_ref.shape, F32)
        leaf_ref[...] = jnp.zeros(leaf_ref.shape, F32)

    pl.when(at < 2)(lambda: work(True))
    pl.when(at >= 2)(lambda: work(False))

    @pl.when(at == pl.num_programs(0) - 1)
    def _():
        for chip in range(chips):
            end = jnp.concatenate([small_ref[chip * tail : (chip + 1) * tail, :], leaf_ref[chip]], 0)
            out_ref[chip, 2 * TILE : 2 * TILE + tail + half, :] = end.astype(BF16)


def collect_kernel(row_local, slot_ref, parts_ref, out_ref, leaf_ref):
    chips, part_rows, width = parts_ref.shape
    set_rows = part_rows - leaf_ref.shape[0]
    sums = []
    for parity in range(2):
        total = parts_ref[parity].astype(F32)
        for chip in range(parity + 2, chips, 2):
            total = total + parts_ref[chip].astype(F32)
        sums.append(total)
    leaf_ref[...] = sums[0][set_rows:] + sums[1][set_rows:]
    requests = jnp.concatenate([sums[0][:set_rows], sums[1][:set_rows]], 0).astype(BF16)
    gather = gather_of(slot_ref, row_local, out_ref.shape[0])
    out_ref[...] = dot(gather, requests, (0, 0)).astype(BF16)


def return_kernel(row_local, incoming_ref, arrived_ref, out_ref):
    lookup = lookup_of(incoming_ref[...], row_local, out_ref.shape[0] * row_local)
    out_ref[...] = dot(lookup, arrived_ref[...], (1, 0)).reshape(out_ref.shape)


def call(kernel, name, out_shape, in_specs, out_specs, scratch=()):
    return pl.pallas_call(
        kernel, name=name, out_shape=out_shape, in_specs=in_specs, out_specs=out_specs,
        scratch_shapes=list(scratch), compiler_params=PARAMS,
    )


def on_device(
    queries, leaf_kv, grad_out, latent_pages, ancestor_home, ancestor_page, ancestor_count
):
    home_count = lax.axis_size("z") * lax.axis_size("x")
    chips = lax.axis_size("y")
    parity = (lax.axis_index("y") % 2).astype(jnp.int32).reshape(1)
    core = lax.axis_index("core").astype(jnp.int32).reshape(1)
    tok_rows, head_local, width = queries.shape
    latent = grad_out.shape[2]
    leaf_count, anc_slots = ancestor_home.shape
    leaf_len = tok_rows // leaf_count
    page_local, row_local = latent_pages.shape[:2]
    live_count = leaf_count // 2 * (anc_slots + 1)
    set_rows = live_count // 2 * row_local
    slot_rows = home_count * CAPACITY * row_local
    block_rows = leaf_len * head_local
    pair_width = -(-(latent + width) // 128) * 128
    swap = [(0, 1), (1, 0)]
    neighbours = [(i, i ^ 1) for i in range(chips)]
    shape = jax.ShapeDtypeStruct

    with jax.named_scope("plan"):
        half = leaf_count // 2
        kept, given, slots, wanted = pl.pallas_call(
            plan_kernel,
            name="plan",
            in_specs=[SMEM] + [pl.BlockSpec(memory_space=pl.ANY)] * 3,
            out_specs=[SMEM, SMEM, SMEM, VMEM],
            out_shape=[
                shape((half + 1,), jnp.int32),
                shape((half + 1,), jnp.int32),
                shape((live_count + 1,), jnp.int32),
                shape((home_count, CAPACITY), jnp.int32),
            ],
            scratch_shapes=[
                pltpu.SMEM((home_count,), jnp.int32),
                pltpu.SMEM((anc_slots, leaf_count), jnp.int32),
                pltpu.SMEM((anc_slots, leaf_count), jnp.int32),
                pltpu.SMEM((leaf_count,), jnp.int32),
                pltpu.SemaphoreType.DMA((3,)),
            ],
            compiler_params=pltpu.CompilerParams(vmem_limit_bytes=56 * 1024 * 1024),
        )(parity, ancestor_home.T, ancestor_page.T, ancestor_count)

    with jax.named_scope("offsets"):
        incoming = lax.all_to_all(wanted, HOME, split_axis=0, concat_axis=0, tiled=True)

    with jax.named_scope("pair"):
        leaf_queries = queries.reshape(leaf_count, block_rows, width)
        leaf_grad_out = grad_out.reshape(leaf_count, block_rows, latent)
        def pick(leaves, name):
            return pl.pallas_call(
                pick_kernel,
                grid_spec=pltpu.PrefetchScalarGridSpec(
                    num_scalar_prefetch=1,
                    grid=(half,),
                    in_specs=[
                        pl.BlockSpec((1, block_rows, width), lambda i, o: (o[i], 0, 0)),
                        pl.BlockSpec((1, block_rows, latent), lambda i, o: (o[i], 0, 0)),
                    ],
                    out_specs=pl.BlockSpec((1, block_rows, pair_width), lambda i, o: (i, 0, 0)),
                ),
                out_shape=shape((half, block_rows, pair_width), BF16),
                compiler_params=PARAMS,
                name=name,
            )(leaves, leaf_queries, leaf_grad_out)

        leaving = pick(given, "pick_given")
        pages = latent_pages.reshape(page_local * row_local, width)
        pages, leaving = lax.optimization_barrier((pages, leaving))
        theirs = lax.ppermute(
            lax.optimization_barrier((leaving, incoming))[0], "y", neighbours
        )
        ours = pick(kept, "pick_kept")
        blocks = [ours, lax.ppermute(ours, "core", swap), theirs, lax.ppermute(theirs, "core", swap)]

    with jax.named_scope("fetch"):
        served = call(
            lambda *refs: serve_kernel(row_local, *refs), "serve",
            shape((home_count, CAPACITY * row_local, width), BF16), [VMEM, VMEM], VMEM,
        )(incoming, pages)
        returned = lax.all_to_all(served, HOME, split_axis=0, concat_axis=0, tiled=True)
        leaving_pages = call(
            lambda *refs: compact_kernel(row_local, *refs), "compact",
            shape((chips, set_rows, width), BF16), [SMEM, VMEM], VMEM,
        )(slots, returned.reshape(slot_rows, width))

    with jax.named_scope("spread"):
        mine = lax.all_to_all(leaving_pages, "y", split_axis=0, concat_axis=0, tiled=True)

    with jax.named_scope("attend"):
        rows = 4 * block_rows
        most_keys = chips * TILE + leaf_len // 2
        block = pl.BlockSpec((1, block_rows, pair_width), lambda i, *s: (i, 0, 0))
        partial = pl.BlockSpec((1, most_keys, rows), lambda i, *s: (i, 0, 0))
        stat = pl.BlockSpec((1, 8, rows), lambda i, *s: (i, 0, 0))
        partial_shape = shape((4, most_keys, rows), F32)
        raised, grad_weights, stats = pl.pallas_call(
            lambda *refs: scores_kernel(latent, *refs),
            name="scores",
            grid_spec=pltpu.PrefetchScalarGridSpec(
                num_scalar_prefetch=2,
                grid=(4,),
                in_specs=[
                    pl.BlockSpec((chips, set_rows, width), lambda i, *s: (0, 0, 0)),
                    pl.BlockSpec((leaf_len, width), lambda i, order, core: (order[i], 0)),
                ] + [block] * 4,
                out_specs=[partial, partial, stat],
            ),
            out_shape=[partial_shape, partial_shape, shape((4, 8, rows), F32)],
            compiler_params=PARAMS,
        )(kept, core, mine, leaf_kv, *blocks)
        other_stats = lax.ppermute(stats, "core", swap)
        part_shape = (chips, set_rows + leaf_len // 2, width)
        part = pl.pallas_call(
            lambda *refs: grads_kernel(latent, *refs),
            name="grads",
            grid_spec=pltpu.PrefetchScalarGridSpec(
                num_scalar_prefetch=1,
                grid=(4,),
                in_specs=[stat, stat] + [block] * 4 + [partial, partial],
                out_specs=pl.BlockSpec(part_shape, lambda i, *s: (0, 0, 0)),
                scratch_shapes=[
                    pltpu.VMEM((chips * (set_rows - 2 * TILE), width), F32),
                    pltpu.VMEM((leaf_count, leaf_len // 2, width), F32),
                ],
            ),
            out_shape=shape(part_shape, BF16),
            compiler_params=PARAMS,
        )(kept, stats, other_stats, *blocks, raised, grad_weights)

    with jax.named_scope("collect"):
        parts = lax.all_to_all(part, "y", split_axis=0, concat_axis=0, tiled=True)
        outbound, leaf_grads = call(
            lambda *refs: collect_kernel(row_local, *refs), "collect",
            [shape((slot_rows, width), BF16), shape((leaf_len // 2, width), F32)],
            [SMEM, VMEM], [VMEM, VMEM],
        )(slots, parts)

    with jax.named_scope("home"):
        arrived = lax.all_to_all(
            outbound.reshape(home_count, CAPACITY * row_local, width),
            HOME, split_axis=0, concat_axis=0, tiled=True,
        )
        page_grads = call(
            lambda *refs: return_kernel(row_local, *refs), "return",
            shape((page_local, row_local, width), F32), [VMEM, VMEM], VMEM,
        )(incoming, arrived.reshape(slot_rows, width))
    return page_grads, leaf_grads


def solution(mesh):
    home_count, head_count = mesh.devices.shape
    side = math.isqrt(home_count)
    split = Mesh(
        mesh.devices.reshape(side, home_count // side, head_count // 2, 2), ("z", "x", "y", "core")
    )
    head = ("y", "core")
    placed = (
        P(HOME, head, None),
        P(HOME, None),
        P(HOME, head, None),
        P(HOME, head, None),
        P(HOME, None),
        P(HOME, None),
        P(HOME),
    )
    return jax.shard_map(
        on_device,
        mesh=split,
        in_specs=placed,
        out_specs=(P(HOME, head, None), P(HOME + head, None)),
        check_vma=False,
    )
```

```python
import math

import jax
import jax.numpy as jnp
from jax import lax
from jax.experimental import pallas as pl
from jax.experimental.pallas import tpu as pltpu
from jax.sharding import Mesh
from jax.sharding import PartitionSpec as P

softmax_scale = 192.0 ** (-0.5)
BF16 = jnp.bfloat16
F32 = jnp.float32
HOME = ("z", "x")
CAPACITY = 2
TILE = 16
VMEM = pl.BlockSpec(memory_space=pltpu.VMEM)
SMEM = pl.BlockSpec(memory_space=pltpu.SMEM)
PARAMS = pltpu.CompilerParams(vmem_limit_bytes=32 * 1024 * 1024)


def iota(shape, dim):
    return lax.broadcasted_iota(jnp.int32, shape, dim)


def dot(a, b, contract):
    return lax.dot_general(a, b, ((contract[:1], contract[1:]), ((), ())), preferred_element_type=F32)


def plan_kernel(
    parity_ref, home_hbm, page_hbm, count_hbm, kept_ref, given_ref, slot_ref, wanted_ref, seen,
    home_ref, page_ref, count_ref, sems,
):
    copies = [
        pltpu.make_async_copy(source, target, sems.at[at])
        for at, (source, target) in enumerate(
            ((home_hbm, home_ref), (page_hbm, page_ref), (count_hbm, count_ref))
        )
    ]
    for copy in copies:
        copy.start()
    for home in range(seen.shape[0]):
        seen[home] = 0
    for copy in copies:
        copy.wait()
    anc_slots, leaf_count = home_ref.shape
    set_size = 2 * anc_slots + 2
    live_count = slot_ref.shape[0] - 1
    spare = kept_ref.shape[0] - 1
    row, column = iota(wanted_ref.shape, 0), iota(wanted_ref.shape, 1)
    wanted = jnp.zeros(wanted_ref.shape, jnp.int32)
    big_seen = small_seen = jnp.int32(0)
    for leaf in range(leaf_count):
        count = count_ref[leaf]
        big = jnp.where(count > 1, 1, 0)
        set_at = jnp.where(big == 1, big_seen // 2, small_seen // 2)
        place = jnp.where(big == 1, big_seen % 2, 2 + small_seen % 2)
        keep = set_at == parity_ref[0]
        kept_ref[jnp.where(keep, place, spare)] = leaf
        given_ref[jnp.where(keep, spare, place)] = leaf
        first = set_at * set_size + jnp.where(
            big == 1, place * anc_slots, 2 * anc_slots + small_seen % 2
        )
        for slot in range(anc_slots):
            live = jnp.where(slot < count, 1, 0)
            home = home_ref[slot, leaf]
            rank = seen[home]
            seen[home] = rank + live
            slot_ref[jnp.where(live == 1, first + slot, live_count)] = home * CAPACITY + rank
            value = page_ref[slot, leaf] + 1
            at = jnp.where(live == 1, home * CAPACITY + rank, -1)
            wanted = jnp.where(row * CAPACITY + column == at, value, wanted)
        big_seen += big
        small_seen += 1 - big
    wanted_ref[...] = wanted


def lookup_of(incoming, row_local, page_rows):
    home_count = incoming.shape[0]
    slot_rows = home_count * CAPACITY * row_local
    per_home = CAPACITY * row_local
    spread = (iota((home_count, slot_rows), 1) // per_home == iota((home_count, slot_rows), 0)).astype(BF16)
    asked = dot(incoming.astype(F32).astype(BF16), spread, (0, 0)).astype(jnp.int32)
    column = iota((1, slot_rows), 1)
    asked = jnp.where((column % per_home) // row_local == 0, asked[:1], asked[1:])
    wanted_row = jnp.where(asked > 0, (asked - 1) * row_local + column % row_local, -1)
    return (iota((page_rows, slot_rows), 0) == wanted_row).astype(BF16)


def serve_kernel(row_local, incoming_ref, pages_ref, out_ref):
    lookup = lookup_of(incoming_ref[...], row_local, pages_ref.shape[0])
    out_ref[...] = dot(lookup, pages_ref[...], (0, 0)).astype(BF16).reshape(out_ref.shape)


def gather_of(slot_ref, row_local, slot_rows):
    live_count = slot_ref.shape[0] - 1
    shape = (live_count * row_local, slot_rows)
    row = iota((shape[0], 1), 0)
    target = jnp.zeros((shape[0], 1), jnp.int32)
    for at in range(live_count):
        target = jnp.where(row // row_local == at, slot_ref[at] * row_local, target)
    return (iota(shape, 1) == target + row % row_local).astype(BF16)


def compact_kernel(row_local, slot_ref, returned_ref, out_ref):
    slot_rows, width = returned_ref.shape
    chips, set_rows, _ = out_ref.shape
    fetched = dot(gather_of(slot_ref, row_local, slot_rows), returned_ref[...], (1, 0))
    sets = [fetched[:set_rows].astype(BF16), fetched[set_rows:].astype(BF16)]
    for chip in range(chips):
        out_ref[chip] = sets[chip % 2]


def pick_kernel(order_ref, query_ref, grad_ref, out_ref):
    latent, width = grad_ref.shape[2], query_ref.shape[2]
    out_ref[0, :, :latent] = grad_ref[0]
    blank = jnp.zeros((out_ref.shape[1], out_ref.shape[2] - latent - width), BF16)
    out_ref[0, :, latent:] = jnp.concatenate([query_ref[0], blank], 1)


def keys_of(mine_ref, at):
    chips, set_rows, width = mine_ref.shape
    tail = set_rows - 2 * TILE
    span = TILE if at < 2 else tail
    start = at * TILE if at < 2 else 2 * TILE
    return mine_ref[:, start : start + span, :].reshape(chips * span, width)


def start_rows(block_refs, held, sems):
    copies = [
        [pltpu.make_async_copy(ref.at[at], held.at[b, at], sems.at[b, at]) for b, ref in enumerate(block_refs)]
        for at in range(4)
    ]
    for of_leaf in copies:
        for copy in of_leaf:
            copy.start()
    return copies


def stacked_of(held, at, latent, width):
    count, _, block_rows, _ = held.shape
    queries = [held[b, at, :, latent : latent + width] for b in range(count)]
    grads = [held[b, at, :, :latent] for b in range(count)]
    blank = jnp.zeros((count * block_rows, width - latent), BF16)
    return jnp.concatenate(queries + [jnp.concatenate([jnp.concatenate(grads, 0), blank], 1)], 0)


def scores_kernel(
    latent, leaf_len, order_ref, core_ref, mine_ref, own_ref, b0_ref, b1_ref, b2_ref, b3_ref,
    big_raised, big_grad, small_raised, small_grad, stats_ref, held, sems,
):
    width = mine_ref.shape[2]
    copies = start_rows((b0_ref, b1_ref, b2_ref, b3_ref), held, sems)
    block_rows = b0_ref.shape[1]
    rows = held.shape[0] * block_rows
    half = leaf_len // 2
    tail = mine_ref.shape[1] - 2 * TILE
    page_rows = TILE // 4
    for at in range(4):
        own_rows = pl.ds(pl.multiple_of(order_ref[at] * leaf_len, leaf_len), leaf_len)
        own = own_ref[own_rows, :].astype(F32)
        own = jnp.where(core_ref[0] == 0, own[:half], own[half:]).astype(BF16)
        pages = keys_of(mine_ref, at)
        paged = pages.shape[0]
        keys = jnp.concatenate([pages, own], 0)
        for copy in copies[at]:
            copy.wait()
        products = dot(keys, stacked_of(held, at, latent, width), (1, 1))
        key_at = iota((paged + half, rows), 0)
        token_at = iota((paged + half, rows), 1) % block_rows // (block_rows // leaf_len)
        strange = 0 if at < 2 else jnp.abs(key_at % tail // page_rows - (at - 2))
        late = jnp.maximum(key_at - paged + half * core_ref[0] - token_at, 0)
        gap = jnp.where(key_at < paged, strange, late)
        scores = jnp.where(gap == 0, softmax_scale * products[:, :rows], -jnp.inf)
        grad_weights = products[:, rows:]
        top = jnp.max(scores, 0, keepdims=True)
        raised = jnp.exp(scores - top)
        total = jnp.sum(raised, 0, keepdims=True)
        weighted = jnp.sum(raised * grad_weights, 0, keepdims=True)
        stats_ref[at] = jnp.concatenate([top, total, weighted, jnp.zeros((5, rows), F32)], 0)
        raised_ref, grad_ref = (big_raised, big_grad) if at < 2 else (small_raised, small_grad)
        raised_ref[at % 2] = raised
        grad_ref[at % 2] = grad_weights


def grads_kernel(
    latent, leaf_len, order_ref, mine_stats, other_stats, b0_ref, b1_ref, b2_ref, b3_ref,
    big_raised, big_grad, small_raised, small_grad, out_ref, held, sems,
):
    chips, _, width = out_ref.shape
    copies = start_rows((b0_ref, b1_ref, b2_ref, b3_ref), held, sems)
    block_rows = b0_ref.shape[1]
    half = leaf_len // 2
    small = None
    leaf_parts = []

    def swapped(at):
        cut = [other_stats[at, :, i * block_rows : (i + 1) * block_rows] for i in (1, 0, 3, 2)]
        return jnp.concatenate(cut, 1)

    for at in range(4):
        there = swapped(at)
        top, top_other = mine_stats[at, 0:1, :], there[0:1]
        most = jnp.maximum(top, top_other)
        factor, factor_other = jnp.exp(top - most), jnp.exp(top_other - most)
        total = factor * mine_stats[at, 1:2, :] + factor_other * there[1:2]
        weighted = factor * mine_stats[at, 2:3, :] + factor_other * there[2:3]
        row_delta = weighted / total
        raised_ref, grad_ref = (big_raised, big_grad) if at < 2 else (small_raised, small_grad)
        weights = raised_ref[at % 2] * (factor / total)
        dscore = softmax_scale * (weights * (grad_ref[at % 2] - row_delta))
        left = jnp.concatenate([dscore.astype(BF16), weights.astype(BF16)], 1)
        for copy in copies[at]:
            copy.wait()
        key_grads = dot(left, stacked_of(held, at, latent, width), (1, 0))
        paged = key_grads.shape[0] - half
        if at < 2:
            out_ref[:, at * TILE : (at + 1) * TILE, :] = (
                key_grads[:paged].astype(BF16).reshape(chips, TILE, width)
            )
        else:
            small = key_grads[:paged] if small is None else small + key_grads[:paged]
        leaf_parts.append((order_ref[at], key_grads[paged:]))
    tail = small.shape[0] // chips
    for chip in range(chips):
        own = jnp.zeros((half, width), F32)
        for leaf, part in leaf_parts:
            own = own + jnp.where(leaf == chip, part, 0.0)
        end = jnp.concatenate([small[chip * tail : (chip + 1) * tail], own], 0)
        out_ref[chip, 2 * TILE : 2 * TILE + tail + half, :] = end.astype(BF16)


def collect_kernel(row_local, slot_ref, parts_ref, out_ref, leaf_ref):
    chips, part_rows, width = parts_ref.shape
    set_rows = part_rows - leaf_ref.shape[0]
    sums = []
    for parity in range(2):
        total = parts_ref[parity].astype(F32)
        for chip in range(parity + 2, chips, 2):
            total = total + parts_ref[chip].astype(F32)
        sums.append(total)
    leaf_ref[...] = sums[0][set_rows:] + sums[1][set_rows:]
    requests = jnp.concatenate([sums[0][:set_rows], sums[1][:set_rows]], 0).astype(BF16)
    gather = gather_of(slot_ref, row_local, out_ref.shape[0])
    out_ref[...] = dot(gather, requests, (0, 0)).astype(BF16)


def return_kernel(row_local, incoming_ref, arrived_ref, out_ref):
    lookup = lookup_of(incoming_ref[...], row_local, out_ref.shape[0] * row_local)
    out_ref[...] = dot(lookup, arrived_ref[...], (1, 0)).reshape(out_ref.shape)


def call(kernel, name, out_shape, in_specs, out_specs, scratch=()):
    return pl.pallas_call(
        kernel, name=name, out_shape=out_shape, in_specs=in_specs, out_specs=out_specs,
        scratch_shapes=list(scratch), compiler_params=PARAMS,
    )


def on_device(
    queries, leaf_kv, grad_out, latent_pages, ancestor_home, ancestor_page, ancestor_count
):
    home_count = lax.axis_size("z") * lax.axis_size("x")
    chips = lax.axis_size("y")
    parity = (lax.axis_index("y") % 2).astype(jnp.int32).reshape(1)
    core = lax.axis_index("core").astype(jnp.int32).reshape(1)
    tok_rows, head_local, width = queries.shape
    latent = grad_out.shape[2]
    leaf_count, anc_slots = ancestor_home.shape
    leaf_len = tok_rows // leaf_count
    page_local, row_local = latent_pages.shape[:2]
    live_count = leaf_count // 2 * (anc_slots + 1)
    set_rows = live_count // 2 * row_local
    slot_rows = home_count * CAPACITY * row_local
    block_rows = leaf_len * head_local
    pair_width = -(-(latent + width) // 128) * 128
    swap = [(0, 1), (1, 0)]
    neighbours = [(i, i ^ 1) for i in range(chips)]
    shape = jax.ShapeDtypeStruct

    with jax.named_scope("plan"):
        half = leaf_count // 2
        kept, given, slots, wanted = pl.pallas_call(
            plan_kernel,
            name="plan",
            in_specs=[SMEM] + [pl.BlockSpec(memory_space=pl.ANY)] * 3,
            out_specs=[SMEM, SMEM, SMEM, VMEM],
            out_shape=[
                shape((half + 1,), jnp.int32),
                shape((half + 1,), jnp.int32),
                shape((live_count + 1,), jnp.int32),
                shape((home_count, CAPACITY), jnp.int32),
            ],
            scratch_shapes=[
                pltpu.SMEM((home_count,), jnp.int32),
                pltpu.SMEM((anc_slots, leaf_count), jnp.int32),
                pltpu.SMEM((anc_slots, leaf_count), jnp.int32),
                pltpu.SMEM((leaf_count,), jnp.int32),
                pltpu.SemaphoreType.DMA((3,)),
            ],
            compiler_params=pltpu.CompilerParams(vmem_limit_bytes=56 * 1024 * 1024),
        )(parity, ancestor_home.T, ancestor_page.T, ancestor_count)

    with jax.named_scope("offsets"):
        incoming = lax.all_to_all(wanted, HOME, split_axis=0, concat_axis=0, tiled=True)

    with jax.named_scope("pair"):
        leaf_queries = queries.reshape(leaf_count, block_rows, width)
        leaf_grad_out = grad_out.reshape(leaf_count, block_rows, latent)
        def pick(leaves, name):
            return pl.pallas_call(
                pick_kernel,
                grid_spec=pltpu.PrefetchScalarGridSpec(
                    num_scalar_prefetch=1,
                    grid=(half,),
                    in_specs=[
                        pl.BlockSpec((1, block_rows, width), lambda i, o: (o[i], 0, 0)),
                        pl.BlockSpec((1, block_rows, latent), lambda i, o: (o[i], 0, 0)),
                    ],
                    out_specs=pl.BlockSpec((1, block_rows, pair_width), lambda i, o: (i, 0, 0)),
                ),
                out_shape=shape((half, block_rows, pair_width), BF16),
                compiler_params=PARAMS,
                name=name,
            )(leaves, leaf_queries, leaf_grad_out)

        leaving = pick(given, "pick_given")
        pages = latent_pages.reshape(page_local * row_local, width)
        pages, leaving = lax.optimization_barrier((pages, leaving))
        theirs = lax.ppermute(
            lax.optimization_barrier((leaving, incoming))[0], "y", neighbours
        )
        ours = pick(kept, "pick_kept")
        blocks = [ours, lax.ppermute(ours, "core", swap), theirs, lax.ppermute(theirs, "core", swap)]

    with jax.named_scope("fetch"):
        served = call(
            lambda *refs: serve_kernel(row_local, *refs), "serve",
            shape((home_count, CAPACITY * row_local, width), BF16), [VMEM, VMEM], VMEM,
        )(incoming, pages)
        returned = lax.all_to_all(served, HOME, split_axis=0, concat_axis=0, tiled=True)
        leaving_pages = call(
            lambda *refs: compact_kernel(row_local, *refs), "compact",
            shape((chips, set_rows, width), BF16), [SMEM, VMEM], VMEM,
        )(slots, returned.reshape(slot_rows, width))

    with jax.named_scope("spread"):
        mine = lax.all_to_all(leaving_pages, "y", split_axis=0, concat_axis=0, tiled=True)

    with jax.named_scope("attend"):
        rows = 4 * block_rows
        in_place = pl.BlockSpec(memory_space=pl.ANY)
        row_scratch = [
            pltpu.VMEM((4, 4, block_rows, pair_width), BF16), pltpu.SemaphoreType.DMA((4, 4))
        ]
        tail = set_rows - 2 * TILE
        big_shape = shape((2, chips * TILE + leaf_len // 2, rows), F32)
        small_shape = shape((2, chips * tail + leaf_len // 2, rows), F32)
        *partial, stats = call(
            lambda *refs: scores_kernel(latent, leaf_len, *refs), "scores",
            [big_shape, big_shape, small_shape, small_shape, shape((4, 8, rows), F32)],
            [SMEM] * 2 + [VMEM] * 2 + [in_place] * 4, [VMEM] * 5, row_scratch,
        )(kept, core, mine, leaf_kv, *blocks)
        other_stats = lax.ppermute(stats, "core", swap)
        part = call(
            lambda *refs: grads_kernel(latent, leaf_len, *refs), "grads",
            shape((chips, set_rows + leaf_len // 2, width), BF16), [SMEM] + [VMEM] * 2 + [in_place] * 4 + [VMEM] * 4, VMEM,
            row_scratch,
        )(kept, stats, other_stats, *blocks, *partial)

    with jax.named_scope("collect"):
        parts = lax.all_to_all(part, "y", split_axis=0, concat_axis=0, tiled=True)
        outbound, leaf_grads = call(
            lambda *refs: collect_kernel(row_local, *refs), "collect",
            [shape((slot_rows, width), BF16), shape((leaf_len // 2, width), F32)],
            [SMEM, VMEM], [VMEM, VMEM],
        )(slots, parts)

    with jax.named_scope("home"):
        arrived = lax.all_to_all(
            outbound.reshape(home_count, CAPACITY * row_local, width),
            HOME, split_axis=0, concat_axis=0, tiled=True,
        )
        page_grads = call(
            lambda *refs: return_kernel(row_local, *refs), "return",
            shape((page_local, row_local, width), F32), [VMEM, VMEM], VMEM,
        )(incoming, arrived.reshape(slot_rows, width))
    return page_grads, leaf_grads


def solution(mesh):
    home_count, head_count = mesh.devices.shape
    side = math.isqrt(home_count)
    split = Mesh(
        mesh.devices.reshape(side, home_count // side, head_count // 2, 2), ("z", "x", "y", "core")
    )
    head = ("y", "core")
    placed = (
        P(HOME, head, None),
        P(HOME, None),
        P(HOME, head, None),
        P(HOME, head, None),
        P(HOME, None),
        P(HOME, None),
        P(HOME),
    )
    return jax.shard_map(
        on_device,
        mesh=split,
        in_specs=placed,
        out_specs=(P(HOME, head, None), P(HOME + head, None)),
        check_vma=False,
    )
```

```python
import math

import jax
import jax.numpy as jnp
from jax import lax
from jax.experimental import pallas as pl
from jax.experimental.pallas import tpu as pltpu
from jax.sharding import Mesh
from jax.sharding import PartitionSpec as P

softmax_scale = 192.0 ** (-0.5)
BF16 = jnp.bfloat16
F32 = jnp.float32
HOME = ("z", "x")
CAPACITY = 2
TILE = 16
VMEM = pl.BlockSpec(memory_space=pltpu.VMEM)
SMEM = pl.BlockSpec(memory_space=pltpu.SMEM)
PARAMS = pltpu.CompilerParams(vmem_limit_bytes=32 * 1024 * 1024)


def iota(shape, dim):
    return lax.broadcasted_iota(jnp.int32, shape, dim)


def dot(a, b, contract):
    return lax.dot_general(a, b, ((contract[:1], contract[1:]), ((), ())), preferred_element_type=F32)


def plan_kernel(
    parity_ref, home_hbm, page_hbm, count_hbm, kept_ref, given_ref, slot_ref, wanted_ref, seen,
    home_ref, page_ref, count_ref, sems,
):
    copies = [
        pltpu.make_async_copy(source, target, sems.at[at])
        for at, (source, target) in enumerate(
            ((home_hbm, home_ref), (page_hbm, page_ref), (count_hbm, count_ref))
        )
    ]
    for copy in copies:
        copy.start()
    for home in range(seen.shape[0]):
        seen[home] = 0
    for copy in copies:
        copy.wait()
    anc_slots, leaf_count = home_ref.shape
    set_size = 2 * anc_slots + 2
    live_count = slot_ref.shape[0] - 1
    spare = kept_ref.shape[0] - 1
    row, column = iota(wanted_ref.shape, 0), iota(wanted_ref.shape, 1)
    wanted = jnp.zeros(wanted_ref.shape, jnp.int32)
    big_seen = small_seen = jnp.int32(0)
    for leaf in range(leaf_count):
        count = count_ref[leaf]
        big = jnp.where(count > 1, 1, 0)
        set_at = jnp.where(big == 1, big_seen // 2, small_seen // 2)
        place = jnp.where(big == 1, big_seen % 2, 2 + small_seen % 2)
        keep = set_at == parity_ref[0]
        kept_ref[jnp.where(keep, place, spare)] = leaf
        given_ref[jnp.where(keep, spare, place)] = leaf
        first = set_at * set_size + jnp.where(
            big == 1, place * anc_slots, 2 * anc_slots + small_seen % 2
        )
        for slot in range(anc_slots):
            live = jnp.where(slot < count, 1, 0)
            home = home_ref[slot, leaf]
            rank = seen[home]
            seen[home] = rank + live
            slot_ref[jnp.where(live == 1, first + slot, live_count)] = home * CAPACITY + rank
            value = page_ref[slot, leaf] + 1
            at = jnp.where(live == 1, home * CAPACITY + rank, -1)
            wanted = jnp.where(row * CAPACITY + column == at, value, wanted)
        big_seen += big
        small_seen += 1 - big
    wanted_ref[...] = wanted


def lookup_of(incoming, row_local, page_rows):
    home_count = incoming.shape[0]
    slot_rows = home_count * CAPACITY * row_local
    per_home = CAPACITY * row_local
    spread = (iota((home_count, slot_rows), 1) // per_home == iota((home_count, slot_rows), 0)).astype(BF16)
    asked = dot(incoming.astype(F32).astype(BF16), spread, (0, 0)).astype(jnp.int32)
    column = iota((1, slot_rows), 1)
    asked = jnp.where((column % per_home) // row_local == 0, asked[:1], asked[1:])
    wanted_row = jnp.where(asked > 0, (asked - 1) * row_local + column % row_local, -1)
    return (iota((page_rows, slot_rows), 0) == wanted_row).astype(BF16)


def serve_kernel(row_local, incoming_ref, pages_ref, out_ref):
    lookup = lookup_of(incoming_ref[...], row_local, pages_ref.shape[0])
    out_ref[...] = dot(lookup, pages_ref[...], (0, 0)).astype(BF16).reshape(out_ref.shape)


def gather_of(slot_ref, row_local, slot_rows):
    live_count = slot_ref.shape[0] - 1
    shape = (live_count * row_local, slot_rows)
    row = iota((shape[0], 1), 0)
    target = jnp.zeros((shape[0], 1), jnp.int32)
    for at in range(live_count):
        target = jnp.where(row // row_local == at, slot_ref[at] * row_local, target)
    return (iota(shape, 1) == target + row % row_local).astype(BF16)


def compact_kernel(row_local, slot_ref, returned_ref, out_ref):
    slot_rows, width = returned_ref.shape
    chips, set_rows, _ = out_ref.shape
    fetched = dot(gather_of(slot_ref, row_local, slot_rows), returned_ref[...], (1, 0))
    sets = [fetched[:set_rows].astype(BF16), fetched[set_rows:].astype(BF16)]
    for chip in range(chips):
        out_ref[chip] = sets[chip % 2]


def pick_kernel(order_ref, query_ref, grad_ref, out_ref):
    latent, width = grad_ref.shape[2], query_ref.shape[2]
    out_ref[0, :, :latent] = grad_ref[0]
    blank = jnp.zeros((out_ref.shape[1], out_ref.shape[2] - latent - width), BF16)
    out_ref[0, :, latent:] = jnp.concatenate([query_ref[0], blank], 1)


def keys_of(mine_ref, at):
    chips, set_rows, width = mine_ref.shape
    tail = set_rows - 2 * TILE
    span = TILE if at < 2 else tail
    start = at * TILE if at < 2 else 2 * TILE
    return mine_ref[:, start : start + span, :].reshape(chips * span, width)


def stacked_of(block_refs, at, latent, width):
    queries = [ref[at, :, latent : latent + width] for ref in block_refs]
    grads = [ref[at, :, :latent] for ref in block_refs]
    blank = jnp.zeros((len(grads) * grads[0].shape[0], width - latent), BF16)
    return jnp.concatenate(queries + [jnp.concatenate([jnp.concatenate(grads, 0), blank], 1)], 0)


def scores_kernel(
    latent, leaf_len, order_ref, core_ref, mine_ref, own_ref, b0_ref, b1_ref, b2_ref, b3_ref,
    big_raised, big_grad, small_raised, small_grad, stats_ref,
):
    width = mine_ref.shape[2]
    block_refs = (b0_ref, b1_ref, b2_ref, b3_ref)
    block_rows = b0_ref.shape[1]
    rows = len(block_refs) * block_rows
    half = leaf_len // 2
    tail = mine_ref.shape[1] - 2 * TILE
    page_rows = TILE // 4
    for at in range(4):
        own_rows = pl.ds(pl.multiple_of(order_ref[at] * leaf_len, leaf_len), leaf_len)
        own = own_ref[own_rows, :].astype(F32)
        own = jnp.where(core_ref[0] == 0, own[:half], own[half:]).astype(BF16)
        pages = keys_of(mine_ref, at)
        paged = pages.shape[0]
        keys = jnp.concatenate([pages, own], 0)
        products = dot(keys, stacked_of(block_refs, at, latent, width), (1, 1))
        key_at = iota((paged + half, rows), 0)
        token_at = iota((paged + half, rows), 1) % block_rows // (block_rows // leaf_len)
        strange = 0 if at < 2 else jnp.abs(key_at % tail // page_rows - (at - 2))
        late = jnp.maximum(key_at - paged + half * core_ref[0] - token_at, 0)
        gap = jnp.where(key_at < paged, strange, late)
        scores = jnp.where(gap == 0, softmax_scale * products[:, :rows], -jnp.inf)
        grad_weights = products[:, rows:]
        top = jnp.max(scores, 0, keepdims=True)
        raised = jnp.exp(scores - top)
        total = jnp.sum(raised, 0, keepdims=True)
        weighted = jnp.sum(raised * grad_weights, 0, keepdims=True)
        stats_ref[at] = jnp.concatenate([top, total, weighted, jnp.zeros((5, rows), F32)], 0)
        raised_ref, grad_ref = (big_raised, big_grad) if at < 2 else (small_raised, small_grad)
        raised_ref[at % 2] = raised
        grad_ref[at % 2] = grad_weights


def grads_kernel(
    latent, leaf_len, order_ref, mine_stats, other_stats, b0_ref, b1_ref, b2_ref, b3_ref,
    big_raised, big_grad, small_raised, small_grad, out_ref, leaf_ref,
):
    chips, _, width = out_ref.shape
    block_refs = (b0_ref, b1_ref, b2_ref, b3_ref)
    block_rows = b0_ref.shape[1]
    half = leaf_len // 2
    small = None
    leaf_parts = []

    def swapped(at):
        cut = [other_stats[at, :, i * block_rows : (i + 1) * block_rows] for i in (1, 0, 3, 2)]
        return jnp.concatenate(cut, 1)

    for at in range(4):
        there = swapped(at)
        top, top_other = mine_stats[at, 0:1, :], there[0:1]
        most = jnp.maximum(top, top_other)
        factor, factor_other = jnp.exp(top - most), jnp.exp(top_other - most)
        total = factor * mine_stats[at, 1:2, :] + factor_other * there[1:2]
        weighted = factor * mine_stats[at, 2:3, :] + factor_other * there[2:3]
        row_delta = weighted / total
        raised_ref, grad_ref = (big_raised, big_grad) if at < 2 else (small_raised, small_grad)
        weights = raised_ref[at % 2] * (factor / total)
        dscore = softmax_scale * (weights * (grad_ref[at % 2] - row_delta))
        left = jnp.concatenate([dscore.astype(BF16), weights.astype(BF16)], 1)
        key_grads = dot(left, stacked_of(block_refs, at, latent, width), (1, 0))
        paged = key_grads.shape[0] - half
        if at < 2:
            out_ref[:, at * TILE : (at + 1) * TILE, :] = (
                key_grads[:paged].astype(BF16).reshape(chips, TILE, width)
            )
        else:
            small = key_grads[:paged] if small is None else small + key_grads[:paged]
        leaf_parts.append((order_ref[at], key_grads[paged:]))
    tail = small.shape[0] // chips
    for chip in range(chips):
        own = jnp.zeros((half, width), F32)
        for leaf, part in leaf_parts:
            own = own + jnp.where(leaf == chip, part, 0.0)
        out_ref[chip, 2 * TILE : 2 * TILE + tail, :] = small[chip * tail : (chip + 1) * tail].astype(BF16)
        leaf_ref[chip] = own.astype(BF16)


def collect_kernel(row_local, slot_ref, parts_ref, out_ref):
    chips = parts_ref.shape[0]
    sums = []
    for parity in range(2):
        total = parts_ref[parity].astype(F32)
        for chip in range(parity + 2, chips, 2):
            total = total + parts_ref[chip].astype(F32)
        sums.append(total)
    requests = jnp.concatenate(sums, 0).astype(BF16)
    gather = gather_of(slot_ref, row_local, out_ref.shape[0])
    out_ref[...] = dot(gather, requests, (0, 0)).astype(BF16)


def return_kernel(row_local, incoming_ref, arrived_ref, out_ref):
    lookup = lookup_of(incoming_ref[...], row_local, out_ref.shape[0] * row_local)
    out_ref[...] = dot(lookup, arrived_ref[...], (1, 0)).reshape(out_ref.shape)


def call(kernel, name, out_shape, in_specs, out_specs, scratch=()):
    return pl.pallas_call(
        kernel, name=name, out_shape=out_shape, in_specs=in_specs, out_specs=out_specs,
        scratch_shapes=list(scratch), compiler_params=PARAMS,
    )


def on_device(
    queries, leaf_kv, grad_out, latent_pages, ancestor_home, ancestor_page, ancestor_count
):
    home_count = lax.axis_size("z") * lax.axis_size("x")
    chips = lax.axis_size("y")
    parity = (lax.axis_index("y") % 2).astype(jnp.int32).reshape(1)
    core = lax.axis_index("core").astype(jnp.int32).reshape(1)
    tok_rows, head_local, width = queries.shape
    latent = grad_out.shape[2]
    leaf_count, anc_slots = ancestor_home.shape
    leaf_len = tok_rows // leaf_count
    page_local, row_local = latent_pages.shape[:2]
    live_count = leaf_count // 2 * (anc_slots + 1)
    set_rows = live_count // 2 * row_local
    slot_rows = home_count * CAPACITY * row_local
    block_rows = leaf_len * head_local
    pair_width = -(-(latent + width) // 128) * 128
    swap = [(0, 1), (1, 0)]
    neighbours = [(i, i ^ 1) for i in range(chips)]
    shape = jax.ShapeDtypeStruct

    with jax.named_scope("plan"):
        half = leaf_count // 2
        kept, given, slots, wanted = pl.pallas_call(
            plan_kernel,
            name="plan",
            in_specs=[SMEM] + [pl.BlockSpec(memory_space=pl.ANY)] * 3,
            out_specs=[SMEM, SMEM, SMEM, VMEM],
            out_shape=[
                shape((half + 1,), jnp.int32),
                shape((half + 1,), jnp.int32),
                shape((live_count + 1,), jnp.int32),
                shape((home_count, CAPACITY), jnp.int32),
            ],
            scratch_shapes=[
                pltpu.SMEM((home_count,), jnp.int32),
                pltpu.SMEM((anc_slots, leaf_count), jnp.int32),
                pltpu.SMEM((anc_slots, leaf_count), jnp.int32),
                pltpu.SMEM((leaf_count,), jnp.int32),
                pltpu.SemaphoreType.DMA((3,)),
            ],
            compiler_params=pltpu.CompilerParams(vmem_limit_bytes=56 * 1024 * 1024),
        )(parity, ancestor_home.T, ancestor_page.T, ancestor_count)

    with jax.named_scope("offsets"):
        incoming = lax.all_to_all(wanted, HOME, split_axis=0, concat_axis=0, tiled=True)

    with jax.named_scope("pair"):
        leaf_queries = queries.reshape(leaf_count, block_rows, width)
        leaf_grad_out = grad_out.reshape(leaf_count, block_rows, latent)
        def pick(leaves, name):
            return pl.pallas_call(
                pick_kernel,
                grid_spec=pltpu.PrefetchScalarGridSpec(
                    num_scalar_prefetch=1,
                    grid=(half,),
                    in_specs=[
                        pl.BlockSpec((1, block_rows, width), lambda i, o: (o[i], 0, 0)),
                        pl.BlockSpec((1, block_rows, latent), lambda i, o: (o[i], 0, 0)),
                    ],
                    out_specs=pl.BlockSpec((1, block_rows, pair_width), lambda i, o: (i, 0, 0)),
                ),
                out_shape=shape((half, block_rows, pair_width), BF16),
                compiler_params=PARAMS,
                name=name,
            )(leaves, leaf_queries, leaf_grad_out)

        leaving = pick(given, "pick_given")
        pages = latent_pages.reshape(page_local * row_local, width)
        pages, leaving = lax.optimization_barrier((pages, leaving))
        theirs = lax.ppermute(
            lax.optimization_barrier((leaving, incoming))[0], "y", neighbours
        )
        ours = pick(kept, "pick_kept")
        blocks = [ours, lax.ppermute(ours, "core", swap), theirs, lax.ppermute(theirs, "core", swap)]

    with jax.named_scope("fetch"):
        served = call(
            lambda *refs: serve_kernel(row_local, *refs), "serve",
            shape((home_count, CAPACITY * row_local, width), BF16), [VMEM, VMEM], VMEM,
        )(incoming, pages)
        returned = lax.all_to_all(served, HOME, split_axis=0, concat_axis=0, tiled=True)
        leaving_pages = call(
            lambda *refs: compact_kernel(row_local, *refs), "compact",
            shape((chips, set_rows, width), BF16), [SMEM, VMEM], VMEM,
        )(slots, returned.reshape(slot_rows, width))

    with jax.named_scope("spread"):
        mine = lax.all_to_all(leaving_pages, "y", split_axis=0, concat_axis=0, tiled=True)

    with jax.named_scope("attend"):
        rows = 4 * block_rows
        tail = set_rows - 2 * TILE
        big_shape = shape((2, chips * TILE + leaf_len // 2, rows), F32)
        small_shape = shape((2, chips * tail + leaf_len // 2, rows), F32)
        *partial, stats = call(
            lambda *refs: scores_kernel(latent, leaf_len, *refs), "scores",
            [big_shape, big_shape, small_shape, small_shape, shape((4, 8, rows), F32)],
            [SMEM] * 2 + [VMEM] * 6, [VMEM] * 5,
        )(kept, core, mine, leaf_kv, *blocks)
        other_stats = lax.ppermute(stats, "core", swap)
        part, leaf_part = call(
            lambda *refs: grads_kernel(latent, leaf_len, *refs), "grads",
            [shape((chips, set_rows, width), BF16), shape((chips, leaf_len // 2, width), BF16)],
            [SMEM] + [VMEM] * 10, [VMEM] * 2,
        )(kept, stats, other_stats, *blocks, *partial)

    with jax.named_scope("collect"):
        parts = lax.all_to_all(part, "y", split_axis=0, concat_axis=0, tiled=True)
        outbound = call(
            lambda *refs: collect_kernel(row_local, *refs), "collect",
            shape((slot_rows, width), BF16), [SMEM, VMEM], VMEM,
        )(slots, parts)
        leaf_grads = lax.psum_scatter(leaf_part, "y", scatter_dimension=0, tiled=False).astype(F32)

    with jax.named_scope("home"):
        arrived = lax.all_to_all(
            outbound.reshape(home_count, CAPACITY * row_local, width),
            HOME, split_axis=0, concat_axis=0, tiled=True,
        )
        page_grads = call(
            lambda *refs: return_kernel(row_local, *refs), "return",
            shape((page_local, row_local, width), F32), [VMEM, VMEM], VMEM,
        )(incoming, arrived.reshape(slot_rows, width))
    return page_grads, leaf_grads


def solution(mesh):
    home_count, head_count = mesh.devices.shape
    side = math.isqrt(home_count)
    split = Mesh(
        mesh.devices.reshape(side, home_count // side, head_count // 2, 2), ("z", "x", "y", "core")
    )
    head = ("y", "core")
    placed = (
        P(HOME, head, None),
        P(HOME, None),
        P(HOME, head, None),
        P(HOME, head, None),
        P(HOME, None),
        P(HOME, None),
        P(HOME),
    )
    return jax.shard_map(
        on_device,
        mesh=split,
        in_specs=placed,
        out_specs=(P(HOME, head, None), P(HOME + head, None)),
        check_vma=False,
    )
```
